32 devices in a mesh: dp: 4 (over y, x), ctx: 2 (over core), tensor: 4 (over z).
Axes of the slice: x: 2, y: 2, z: 4, core: 2. Of those that a mesh axis runs over, the one named last changes fastest.
Arguments:
- tokens: bfloat16 [8192, 1024], P(('dp', 'ctx'), 'tensor'), may hold values from -6 to 6
- span_of_slot: int32 [4], replicated, may hold values from 0 to 3, each once
- norm_gain: bfloat16 [2, 1024], replicated, may hold values from 0.25 to 1.75
- norm_bias: bfloat16 [2, 1024], replicated, may hold values from -1 to 1
- qkv_weight: bfloat16 [3, 1024, 1024], P(None, None, 'tensor'), may hold values from -0.25 to 0.25
- qkv_bias: bfloat16 [3, 1024], P(None, 'tensor'), may hold values from -1 to 1
- attn_out_weight: bfloat16 [1024, 1024], P('tensor'), may hold values from -0.75 to 0.75
- out_bias: bfloat16 [2, 1024], P(None, 'tensor'), may hold values from -1 to 1
- mlp_in_weight: bfloat16 [1024, 4096], P(None, 'tensor'), may hold values from -0.1875 to 0.1875
- mlp_in_bias: bfloat16 [4096], P('tensor'), may hold values from -1 to 1
- mlp_out_weight: bfloat16 [4096, 1024], P('tensor'), may hold values from -0.09375 to 0.09375
- cotangent: bfloat16 [8192, 1024], P(('dp', 'ctx'), 'tensor'), may hold values from -6 to 6
Outputs:
- mixed: bfloat16 [8192, 1024], P(('dp', 'ctx'), 'tensor')
- input_grad: float32 [8192, 1024], P(('dp', 'ctx'), 'tensor')
- norm_gain_grad: float32 [2, 1024], P(None, 'tensor')
- norm_bias_grad: float32 [2, 1024], P(None, 'tensor')
- qkv_weight_grad: float32 [3, 1024, 1024], P(None, None, 'tensor')
- qkv_bias_grad: float32 [3, 1024], P(None, 'tensor')
- attn_out_weight_grad: float32 [1024, 1024], P('tensor')
- out_bias_grad: float32 [2, 1024], P(None, 'tensor')
- mlp_in_weight_grad: float32 [1024, 4096], P(None, 'tensor')
- mlp_in_bias_grad: float32 [4096], P('tensor')
- mlp_out_weight_grad: float32 [4096, 1024], P('tensor')
The draws below stay inside these ranges and needn't reach their ends.
Inputs may be any that keep to these rules, and one draw needn't show every extreme that they name: A permutation: slot s, the block s % 2 of the two blocks of 512 rows of every sequence on index s // 2 of ctx, holds the positions span_of_slot[s] * 512 to span_of_slot[s] * 512 + 511 of that sequence.
All inputs are finite; a program needn't handle non-finite values.
Results may differ from the reference program's by a relative error of at most 0.008.
The reference program's roundings to bfloat16 on the way count: a program that leaves them out, or rounds other values in their place, can miss the bound.
Values may be sent and summed in bfloat16 or wider, within the bound.
A program may use at most 192 MiB of HBM per device.

```python
import jax
import jax.numpy as jnp
from jax import lax

D = 1024
HEADS = 16
HEAD = 64
ROT = 16
FF = 4096
LEN = 2048
SEQS = 1
TOKENS = 8192
N_DP = 4
N_CTX = 2


def shard_levels(key, shape, shards, low, top_value):
    gain, own = 1.0, jax.random.fold_in(key, 6)
    for position, parts in shards:
        draws = jnp.exp(jax.random.uniform(jax.random.fold_in(own, position), (parts,), jnp.float32, low / len(shards), top_value / len(shards)))
        gain = gain * jnp.repeat(draws, shape[position] // parts).reshape([-1 if axis == position else 1 for axis in range(len(shape))])
    return gain


def noise(rng, extent, width, bound, cuts=(), kind=jnp.bfloat16):
    level = shard_levels(rng, extent, cuts, -0.22, 0.18) if cuts else 1.0
    entries = jax.random.normal(rng, extent, jnp.float32) * width * level
    return jnp.minimum(jnp.maximum(entries, -bound), bound).astype(kind)


def setup_inputs(seed: int = 0) -> dict:
    splits = jax.random.split(jax.random.key(seed), 13)
    return {
        "tokens": noise(splits[0], (TOKENS, D), 1.0, 6.0, ((0, 8), (1, 4))),
        "span_of_slot": jax.random.permutation(splits[1], 2 * N_CTX).astype(jnp.int32),
        "norm_gain": jnp.clip(1.0 + 0.15 * jax.random.normal(splits[2], (2, D), jnp.float32), 0.25, 1.75).astype(jnp.bfloat16),
        "norm_bias": noise(splits[3], (2, D), 0.2, 1.0),
        "qkv_weight": noise(splits[4], (3, D, D), (D // 2) ** -0.5, 0.25, ((2, 4),)),
        "qkv_bias": noise(splits[5], (3, D), 0.2, 1.0, ((1, 4),)),
        "attn_out_weight": noise(splits[6], (D, D), (D // 16) ** -0.5, 0.75, ((0, 4),)),
        "out_bias": noise(splits[7], (2, D), 0.2, 1.0, ((1, 4),)),
        "mlp_in_weight": noise(splits[8], (D, FF), D ** -0.5, 0.1875, ((1, 4),)),
        "mlp_in_bias": noise(splits[9], (FF,), 0.2, 1.0, ((0, 4),)),
        "mlp_out_weight": noise(splits[10], (FF, D), FF ** -0.5, 0.09375, ((0, 4),)),
        "cotangent": noise(splits[11], (TOKENS, D), 1.0, 6.0, ((0, 8), (1, 4))),
    }


@jax.custom_vjp
def low(v):
    return lax.optimization_barrier(v.astype(jnp.bfloat16)).astype(jnp.float32)

@jax.custom_vjp
def low_back(v):
    return v

def low_keep(v):
    return (low(v), None)

def low_pass(kept, grad):
    return (grad,)

def back_keep(v):
    return (v, None)

def back_low(kept, grad):
    return (low(grad),)
low.defvjp(low_keep, low_pass)
low_back.defvjp(back_keep, back_low)

def norm_rows(full_rows):
    average = lax.optimization_barrier(jnp.mean(full_rows, axis=-1, keepdims=True))
    centred = full_rows - average
    variance = lax.optimization_barrier(jnp.mean(centred * centred, axis=-1, keepdims=True))
    return centred * lax.rsqrt(variance + 1e-05)

def rotation_tables(positions):
    half_rot = ROT // 2
    frequency = 10000.0 ** (-2.0 * jnp.arange(half_rot, dtype=jnp.float32) / ROT)
    angle_rows = positions.astype(jnp.float32)[:, None] * frequency[None, :]
    return (jnp.cos(angle_rows)[:, None, :], jnp.sin(angle_rows)[:, None, :])

def rotate(field, cosine, sine):
    half_rot = cosine.shape[-1]
    lower_part = field[..., :half_rot]
    upper_part = field[..., half_rot:2 * half_rot]
    return jnp.concatenate([lower_part * cosine - upper_part * sine, upper_part * cosine + lower_part * sine, field[..., 2 * half_rot:]], axis=-1)

def reference(tokens, span_of_slot, norm_gain, norm_bias, qkv_weight, qkv_bias, attn_out_weight, out_bias, mlp_in_weight, mlp_in_bias, mlp_out_weight, cotangent):
    span_len = LEN // (2 * N_CTX)
    seq_total = N_DP * SEQS

    def to_sequences(array):
        return array.reshape(N_DP, N_CTX, SEQS, 2 * span_len, D).transpose(0, 2, 1, 3, 4).reshape(seq_total, LEN, D)

    def from_sequences(array):
        return array.reshape(N_DP, SEQS, N_CTX, 2 * span_len, D).transpose(0, 2, 1, 3, 4).reshape(TOKENS, D)
    row_index = jnp.arange(LEN, dtype=jnp.int32)
    slot_index = row_index // (2 * span_len) * 2 + row_index // span_len % 2
    positions = (span_of_slot[slot_index] * span_len + row_index % span_len).astype(jnp.int32)
    cosine, sine = rotation_tables(positions)
    block_rows = min(512, LEN)
    block_count = LEN // block_rows

    def layer(weights, inputs):
        gains, shifts, w_qkv, b_qkv, w_attn, b_out, w_in, b_in, w_mlp = weights
        normed = norm_rows(inputs)
        norm_first = low(normed * gains[0] + shifts[0])
        norm_second = low(normed * gains[1] + shifts[1])
        projected = jnp.einsum('td,cde->cte', norm_first, w_qkv, precision=lax.Precision.HIGHEST) + b_qkv[:, None, :]
        projected = low_back(projected)
        query = low(rotate(projected[0].reshape(LEN, HEADS, HEAD), cosine, sine))
        key_rows = low(rotate(projected[1].reshape(LEN, HEADS, HEAD), cosine, sine))
        value_rows = low(projected[2].reshape(LEN, HEADS, HEAD))

        def attend_block(block):
            query_block, query_pos = block
            raw = low_back(0.125 * jnp.einsum('qhd,khd->hqk', query_block, key_rows, precision=lax.Precision.HIGHEST))
            allowed = positions[None, None, :] <= query_pos[None, :, None]
            weight = jnp.where(allowed, jnp.exp(raw), 0.0)
            mass = lax.optimization_barrier(jnp.sum(weight, axis=-1))
            summed = low_back(jnp.einsum('hqk,khd->qhd', low(weight), value_rows, precision=lax.Precision.HIGHEST))
            return summed / mass.T[:, :, None]
        attended = lax.map(jax.checkpoint(attend_block), (query.reshape(block_count, block_rows, HEADS, HEAD), positions.reshape(block_count, block_rows)))
        attended = low(attended.reshape(LEN, D))
        hidden = low_back(jnp.dot(norm_second, w_in, precision=lax.Precision.HIGHEST) + b_in)
        activated = low(jax.nn.gelu(hidden, approximate=False))
        attn_branch = jnp.dot(attended, w_attn, precision=lax.Precision.HIGHEST) + b_out[0]
        mlp_branch = jnp.dot(activated, w_mlp, precision=lax.Precision.HIGHEST) + b_out[1]
        return inputs + attn_branch + mlp_branch

    def whole(weights, sequences):

        def single(one_seq):
            return layer(weights, one_seq)
        return lax.map(jax.checkpoint(single), sequences)
    params = (norm_gain.astype(jnp.float32), norm_bias.astype(jnp.float32), qkv_weight.astype(jnp.float32), qkv_bias.astype(jnp.float32), attn_out_weight.astype(jnp.float32), out_bias.astype(jnp.float32), mlp_in_weight.astype(jnp.float32), mlp_in_bias.astype(jnp.float32), mlp_out_weight.astype(jnp.float32))
    inputs = to_sequences(tokens.astype(jnp.float32))
    outputs, pull_back = jax.vjp(whole, params, inputs)
    weight_grads, input_grads = pull_back(to_sequences(cotangent.astype(jnp.float32)))
    mixed = from_sequences(outputs).astype(jnp.bfloat16)
    return (mixed, from_sequences(input_grads), weight_grads[0], weight_grads[1], weight_grads[2], weight_grads[3], weight_grads[4], weight_grads[5], weight_grads[6], weight_grads[7], weight_grads[8])
```

```python
import functools

import jax
import jax.numpy as jnp
from jax import lax
from jax.experimental import pallas as pl
from jax.experimental.pallas import tpu as pltpu
from jax.sharding import PartitionSpec as P

HEAD = 64
ROT = 16
LEN = 2048
BF16 = jnp.bfloat16
F32 = jnp.float32


def line_gather(block, axis, pieces):
    size = lax.axis_size(axis)
    me = lax.axis_index(axis)
    width = block.shape[1]
    rows = block.shape[0] // pieces
    gathered = []
    for piece in range(pieces):
        own = block[piece * rows : (piece + 1) * rows]
        rising, falling, below, above = own, own, [], []
        for step in range(size - 1):
            rising = lax.ppermute(rising, axis, [(i, i + 1) for i in range(step, size - 1)])
            falling = lax.ppermute(falling, axis, [(i + 1, i) for i in range(size - 1 - step)])
            below.append(rising)
            above.append(falling)
        side = jnp.concatenate(below[::-1] + [own] + above, axis=1)
        gathered.append(
            lax.dynamic_slice_in_dim(side, (size - 1 - me) * width, size * width, 1)
        )
    return gathered


def line_scatter(terms, axis):
    size = lax.axis_size(axis)
    me = lax.axis_index(axis)
    width = terms.shape[1] // size

    def columns(owner):
        return lax.dynamic_slice_in_dim(terms, jnp.clip(owner, 0, size - 1) * width, width, 1)

    rising = falling = None
    for step in range(1, size):
        reach = size - step
        up, down = columns(me + reach), columns(me - reach)
        if rising is not None:
            up, down = up + rising.astype(F32), down + falling.astype(F32)
        rising = lax.ppermute(
            up.astype(BF16), axis, [(i, i + 1) for i in range(size - 1) if i + reach < size]
        )
        falling = lax.ppermute(
            down.astype(BF16), axis, [(i, i - 1) for i in range(1, size) if i - reach >= 0]
        )
    total = columns(me)
    if rising is not None:
        total = total + rising.astype(F32) + falling.astype(F32)
    return total


def swap(block, axis, bit):
    return lax.ppermute(block, axis, [(i, i ^ bit) for i in range(lax.axis_size(axis))])


def small_sum(block, axes):
    for axis in axes:
        bit = 1
        while bit < lax.axis_size(axis):
            block = block + swap(block, axis, bit)
            bit *= 2
    return block


def weight_sum(term):
    spans, groups = lax.axis_size("ctx"), lax.axis_size("dp")
    if spans != 2:
        return lax.psum(term, ("dp", "ctx"))
    core, chip = lax.axis_index("ctx"), lax.axis_index("dp")
    rows, width = term.shape
    shares = term.reshape(spans, groups, rows // (spans * groups), width)
    given = lax.dynamic_index_in_dim(shares, 1 - core, 0, False).astype(BF16)
    kept = lax.dynamic_index_in_dim(shares, core, 0, False) + swap(given, "ctx", 1).astype(F32)
    own = lax.dynamic_index_in_dim(kept, chip, 0, False)
    low = kept.astype(BF16)
    for bit in range(1, groups):
        own = own + swap(
            lax.dynamic_index_in_dim(low, chip ^ bit, 0, False), "dp", bit
        ).astype(F32)
    own = own.astype(BF16)
    whole = jnp.zeros(low.shape, BF16)
    whole = lax.dynamic_update_index_in_dim(whole, own, chip, 0)
    for bit in range(1, groups):
        whole = lax.dynamic_update_index_in_dim(whole, swap(own, "dp", bit), chip ^ bit, 0)
    other = swap(whole, "ctx", 1)
    first, second = jnp.where(core == 0, whole, other), jnp.where(core == 0, other, whole)
    return jnp.stack([first, second]).astype(F32).reshape(rows, width)


def attention_body(
    heads, chunk, qmax, kmin, q, g, k, v, qpos, kpos, att, dq, dk, dv, e_keep, mass, out, k_head, v_head
):
    block = pl.program_id(1)
    width = q.shape[-1]
    chunks = k.shape[1] // chunk
    lane = lax.broadcasted_iota(jnp.int32, (1, width), 1)
    picks = [((lane >= h * HEAD) & (lane < (h + 1) * HEAD)).astype(F32) for h in range(heads)]

    @pl.when(block == 0)
    def _():
        dk[...] = jnp.zeros_like(dk)
        dv[...] = jnp.zeros_like(dv)
        for h in range(heads):
            k_head[h] = k[0] * picks[h].astype(BF16)
            v_head[h] = v[0] * picks[h].astype(BF16)

    nt = (((1,), (1,)), ((), ()))
    tn = (((0,), (0,)), ((), ()))
    dq[...] = jnp.zeros_like(dq)
    queries = q[0]
    grads = g[0]
    result = jnp.zeros(grads.shape, F32)
    for h in range(heads):
        mass[...] = jnp.zeros_like(mass)
        out[...] = jnp.zeros_like(out)
        for c in range(chunks):
            part = pl.ds(c * chunk, chunk)

            @pl.when(kmin[c] <= qmax[block])
            def _():
                raw = lax.dot_general(queries, k_head[h, part], nt, preferred_element_type=F32)
                e = jnp.where(kpos[:, part] <= qpos[...], jnp.exp(raw), 0.0)
                e_keep[:, part] = e
                mass[...] += jnp.sum(e, axis=1, keepdims=True)
                out[...] += jnp.dot(e.astype(BF16), v_head[h, part], preferred_element_type=F32)

        inverse = 1.0 / mass[...]
        attended = out[...] * inverse
        result = result + attended
        scaled = (grads * inverse).astype(BF16)
        corr = jnp.sum(grads * attended, axis=1, keepdims=True) * inverse
        pick = picks[h].astype(BF16)
        scaled_head = scaled * pick
        q_head = queries * pick
        for c in range(chunks):
            part = pl.ds(c * chunk, chunk)

            @pl.when(kmin[c] <= qmax[block])
            def _():
                e = e_keep[:, part]
                slope = lax.dot_general(scaled, v_head[h, part], nt, preferred_element_type=F32)
                d_raw = (e * (slope - corr)).astype(BF16)
                dq[0] += jnp.dot(d_raw, k_head[h, part], preferred_element_type=F32)
                dk[0, part] += lax.dot_general(d_raw, q_head, tn, preferred_element_type=F32)
                dv[0, part] += lax.dot_general(
                    e.astype(BF16), scaled_head, tn, preferred_element_type=F32
                )

    att[0] = result.astype(BF16)


def attention(q, g, k, v, qpos, kpos):
    seqs, q_rows, width = q.shape
    k_rows = k.shape[1]
    heads = width // HEAD
    block, chunk = min(512, q_rows), min(512, k_rows)
    qmax = jnp.max(qpos.reshape(-1, block), axis=1)
    kmin = jnp.min(kpos.reshape(-1, chunk), axis=1)
    by_block = pl.BlockSpec((1, block, width), lambda s, b: (s, b, 0))
    by_seq = pl.BlockSpec((1, k_rows, width), lambda s, b: (s, 0, 0))
    smem = pl.BlockSpec(memory_space=pltpu.SMEM)
    pairs = seqs * q_rows * k_rows * width
    return pl.pallas_call(
        functools.partial(attention_body, heads, chunk),
        grid=(seqs, q_rows // block),
        in_specs=[
            smem,
            smem,
            by_block,
            by_block,
            by_seq,
            by_seq,
            pl.BlockSpec((block, 1), lambda s, b: (b, 0)),
            pl.BlockSpec((1, k_rows), lambda s, b: (0, 0)),
        ],
        out_specs=[by_block, by_block, by_seq, by_seq],
        out_shape=[
            jax.ShapeDtypeStruct(q.shape, BF16),
            jax.ShapeDtypeStruct(q.shape, F32),
            jax.ShapeDtypeStruct(k.shape, F32),
            jax.ShapeDtypeStruct(k.shape, F32),
        ],
        scratch_shapes=[
            pltpu.VMEM((block, k_rows), F32),
            pltpu.VMEM((block, 1), F32),
            pltpu.VMEM((block, width), F32),
            pltpu.VMEM((heads, k_rows, width), BF16),
            pltpu.VMEM((heads, k_rows, width), BF16),
        ],
        cost_estimate=pl.CostEstimate(
            flops=48 * pairs, bytes_accessed=16 * seqs * k_rows * width, transcendentals=pairs // HEAD
        ),
        compiler_params=pltpu.CompilerParams(vmem_limit_bytes=44 * 2**20),
    )(qmax, kmin, q, g, k, v, qpos[:, None], kpos[None, :])


def norm_forward(full_rows):
    average = jnp.mean(full_rows, axis=-1, keepdims=True)
    centred = full_rows - average
    variance = jnp.mean(centred * centred, axis=-1, keepdims=True)
    inverse_scale = lax.rsqrt(variance + 1e-05)
    return (centred * inverse_scale, inverse_scale)


def rotation_tables(positions, width):
    half_rot = ROT // 2
    dim = jnp.arange(width, dtype=jnp.int32) % HEAD
    frequency = 10000.0 ** (-2.0 * (dim % half_rot).astype(F32) / ROT)
    angle = positions.astype(F32)[:, None] * frequency[None, :]
    cosine = jnp.where(dim < ROT, jnp.cos(angle), 1.0)
    sine = jnp.sin(angle)
    lower = jnp.where(dim < half_rot, sine, 0.0)
    upper = jnp.where((dim >= half_rot) & (dim < ROT), sine, 0.0)
    return lax.optimization_barrier((cosine, lower, upper))


def rotate(field, tables, sign):
    cosine, lower, upper = tables
    half_rot = ROT // 2
    return (
        field * cosine
        - sign * jnp.roll(field, -half_rot, axis=1) * lower
        + sign * jnp.roll(field, half_rot, axis=1) * upper
    )


def local(
    tokens,
    span_of_slot,
    norm_gain,
    norm_bias,
    qkv_weight,
    qkv_bias,
    attn_out_weight,
    out_bias,
    mlp_in_weight,
    mlp_in_bias,
    mlp_out_weight,
    cotangent,
):
    tok_rows, local_width = tokens.shape
    ctx_count = lax.axis_size("ctx")
    span_len = LEN // (2 * ctx_count)
    seq_count = tok_rows // (2 * span_len)
    seq_rows = 2 * span_len
    head_width = qkv_weight.shape[2]
    column_start = lax.axis_index("tensor") * local_width

    full_tokens = jnp.concatenate(line_gather(tokens, "tensor", 2), axis=0)
    full_tokens, late_cotangent = lax.optimization_barrier((full_tokens, cotangent))
    full_grads = jnp.concatenate(line_gather(late_cotangent, "tensor", 2), axis=0)

    slot_table = span_of_slot.reshape(ctx_count, 2)
    offsets = jnp.arange(span_len, dtype=jnp.int32)

    def positions_of(spans):
        return (spans[..., None] * span_len + offsets).reshape(-1)

    own_spans = lax.dynamic_index_in_dim(slot_table, lax.axis_index("ctx"), 0, False)
    query_pos = positions_of(own_spans)
    tables = rotation_tables(jnp.tile(query_pos, seq_count), head_width)

    normed, inverse_scale = norm_forward(full_tokens.astype(F32))
    gains = norm_gain.astype(F32)
    shifts = norm_bias.astype(F32)
    norm_first = (normed * gains[0] + shifts[0]).astype(BF16)
    norm_second = (normed * gains[1] + shifts[1]).astype(BF16)

    projected = [
        jnp.dot(norm_first, qkv_weight[c], preferred_element_type=F32) + qkv_bias[c].astype(F32)
        for c in range(3)
    ]
    query_b = (rotate(projected[0], tables, 1.0).astype(BF16) * BF16(0.125)).reshape(
        seq_count, seq_rows, head_width
    )
    key_value = jnp.stack([rotate(projected[1], tables, 1.0).astype(BF16), projected[2].astype(BF16)])
    if ctx_count == 2:
        other_spans = lax.dynamic_index_in_dim(slot_table, 1 - lax.axis_index("ctx"), 0, False)
        key_pos = positions_of(jnp.concatenate([own_spans, other_spans]))
        shards = [key_value, swap(key_value, "ctx", 1)]
    else:
        key_pos = positions_of(span_of_slot)
        shards = list(lax.all_gather(key_value, "ctx"))
    key_value = jnp.concatenate(
        [shard.reshape(2, seq_count, seq_rows, head_width) for shard in shards], axis=2
    )

    hidden = jnp.dot(norm_second, mlp_in_weight, preferred_element_type=F32) + mlp_in_bias.astype(F32)
    normal_cdf = 0.5 * (1.0 + lax.erf(hidden * 0.7071067811865476))
    density = jnp.exp(-0.5 * hidden * hidden) * 0.3989422804014327
    activated_b, gelu_slope = lax.optimization_barrier(
        ((hidden * normal_cdf).astype(BF16), normal_cdf + hidden * density)
    )

    grad_local = cotangent.astype(F32)
    mlp_out_term = jnp.dot(activated_b.T, full_grads, preferred_element_type=F32)
    mlp_out_grad = weight_sum(mlp_out_term)
    grad_activated = jnp.dot(full_grads, mlp_out_weight.T, preferred_element_type=F32)
    grad_hidden = lax.optimization_barrier((grad_activated * gelu_slope).astype(BF16))
    mlp_in_term = jnp.dot(norm_second.T, grad_hidden, preferred_element_type=F32)
    mlp_in_grad = weight_sum(mlp_in_term)

    grad_attended = jnp.dot(full_grads, attn_out_weight.T, preferred_element_type=F32)
    attended_b, grad_query, grad_key, grad_value = attention(
        query_b,
        grad_attended.reshape(seq_count, seq_rows, head_width),
        key_value[0],
        key_value[1],
        query_pos,
        key_pos,
    )
    attended_b = attended_b.reshape(tok_rows, head_width)

    if ctx_count == 2:

        def to_owner(grad):
            return (grad[:, :seq_rows] + swap(grad[:, seq_rows:], "ctx", 1)).reshape(
                tok_rows, head_width
            )
    else:

        def to_owner(grad):
            shares = grad.reshape(seq_count, ctx_count, seq_rows, head_width).swapaxes(0, 1)
            return lax.psum_scatter(
                shares.reshape(ctx_count * tok_rows, head_width), "ctx", scatter_dimension=0, tiled=True
            )

    attn_out_term = jnp.dot(attended_b.T, full_grads, preferred_element_type=F32)
    attn_out_grad = weight_sum(attn_out_term)
    branch_terms = jnp.dot(attended_b, attn_out_weight, preferred_element_type=F32) + jnp.dot(
        activated_b, mlp_out_weight, preferred_element_type=F32
    )
    branch_sum = line_scatter(branch_terms, "tensor")
    bias_rows = out_bias.astype(F32)
    mixed = (tokens.astype(F32) + branch_sum + bias_rows[0] + bias_rows[1]).astype(BF16)

    second_part = jnp.dot(grad_hidden, mlp_in_weight.T, preferred_element_type=F32)
    grad_proj = [
        rotate(0.125 * grad_query.reshape(tok_rows, head_width), tables, -1.0).astype(BF16),
        rotate(to_owner(grad_key), tables, -1.0).astype(BF16),
        to_owner(grad_value).astype(BF16),
    ]
    grad_proj = lax.optimization_barrier(jnp.concatenate(grad_proj, axis=1))
    qkv_term = jnp.dot(grad_proj.T, norm_first, preferred_element_type=F32)
    qkv_grad = weight_sum(qkv_term)
    flat_weight = qkv_weight.transpose(1, 0, 2).reshape(qkv_weight.shape[1], 3 * head_width)
    first_part = jnp.dot(grad_proj, flat_weight.T, preferred_element_type=F32)

    combined = first_part * gains[0] + second_part * gains[1]
    back_sum = line_scatter(combined, "tensor")
    means = small_sum(
        jnp.stack([jnp.sum(combined, axis=1), jnp.sum(combined * normed, axis=1)]), ("tensor",)
    ) * (1.0 / full_tokens.shape[1])
    own_normed = lax.dynamic_slice_in_dim(normed, column_start, local_width, 1)
    input_grad = grad_local + inverse_scale * (
        back_sum - means[0][:, None] - own_normed * means[1][:, None]
    )

    norm_term = jnp.stack(
        [
            jnp.sum(first_part * normed, axis=0),
            jnp.sum(second_part * normed, axis=0),
            jnp.sum(first_part, axis=0),
            jnp.sum(second_part, axis=0),
        ]
    )
    norm_sum = lax.dynamic_slice_in_dim(
        small_sum(norm_term, ("tensor", "ctx", "dp")), column_start, local_width, 1
    )
    bias_sum = small_sum(
        jnp.concatenate(
            [
                jnp.sum(grad_proj.astype(F32), axis=0),
                jnp.sum(grad_local, axis=0),
                jnp.sum(grad_hidden.astype(F32), axis=0),
            ]
        ),
        ("ctx", "dp"),
    )
    out_bias_grad = bias_sum[3 * head_width : 3 * head_width + local_width]
    return (
        mixed,
        input_grad,
        norm_sum[0:2],
        norm_sum[2:4],
        qkv_grad.reshape(3, head_width, -1).transpose(0, 2, 1),
        bias_sum[: 3 * head_width].reshape(3, head_width),
        attn_out_grad,
        jnp.stack([out_bias_grad, out_bias_grad]),
        mlp_in_grad,
        bias_sum[3 * head_width + local_width :],
        mlp_out_grad,
    )


def solution(mesh):
    placed = (
        P(("dp", "ctx"), "tensor"),
        P(),
        P(),
        P(),
        P(None, None, "tensor"),
        P(None, "tensor"),
        P("tensor", None),
        P(None, "tensor"),
        P(None, "tensor"),
        P("tensor"),
        P("tensor", None),
        P(("dp", "ctx"), "tensor"),
    )
    return jax.shard_map(
        local,
        mesh=mesh,
        in_specs=placed,
        out_specs=(
            P(("dp", "ctx"), "tensor"),
            P(("dp", "ctx"), "tensor"),
            P(None, "tensor"),
            P(None, "tensor"),
            P(None, None, "tensor"),
            P(None, "tensor"),
            P("tensor", None),
            P(None, "tensor"),
            P(None, "tensor"),
            P("tensor"),
            P("tensor", None),
        ),
        check_vma=False,
    )
```

```python
import functools

import jax
import jax.numpy as jnp
from jax import lax
from jax.experimental import pallas as pl
from jax.experimental.pallas import tpu as pltpu
from jax.sharding import PartitionSpec as P

HEAD = 64
ROT = 16
LEN = 2048
BF16 = jnp.bfloat16
F32 = jnp.float32


VMEM = pl.BlockSpec(memory_space=pltpu.VMEM)


def greet(partners):
    barrier = pltpu.get_barrier_semaphore()
    expected = 0
    for exists, device in partners:
        if exists is True:
            pl.semaphore_signal(barrier, inc=1, device_id=device)
            expected = expected + 1
        else:

            @pl.when(exists)
            def _():
                pl.semaphore_signal(barrier, inc=1, device_id=device)

            expected = expected + exists.astype(jnp.int32)
    pl.semaphore_wait(barrier, expected)


def line_partners(size, me):
    return [(me > 0, {"tensor": me - 1}), (me < size - 1, {"tensor": me + 1})]


def gather_body(size, pieces, *refs):
    blocks, wholes = refs[:2], refs[2:4]
    up_send, up_recv, down_send, down_recv, own_sem = refs[4:]
    me = lax.axis_index("tensor")
    rows, width = blocks[0].shape
    rows = rows // pieces
    greet(line_partners(size, me))

    def place(array, owner, piece):
        columns = pl.ds(pl.multiple_of(owner * width, width), width)
        return wholes[array].at[pl.ds(piece * rows, rows), columns]

    def copy(array, piece, step, sign):
        slot = (array * pieces + piece, step)
        send, recv = (up_send, up_recv) if sign > 0 else (down_send, down_recv)
        target = place(array, me - sign * step, piece)
        source = blocks[array].at[pl.ds(piece * rows, rows)] if step == 0 else target
        return pltpu.make_async_remote_copy(
            src_ref=source,
            dst_ref=target,
            send_sem=send.at[slot],
            recv_sem=recv.at[slot],
            device_id={"tensor": me + sign},
        )

    def arrival(array, piece, step, sign):
        slot = (array * pieces + piece, step)
        send, recv = (up_send, up_recv) if sign > 0 else (down_send, down_recv)
        target = place(array, me - sign * (step + 1), piece)
        return pltpu.make_async_remote_copy(
            src_ref=target,
            dst_ref=target,
            send_sem=send.at[slot],
            recv_sem=recv.at[slot],
            device_id={"tensor": me - sign},
        )

    own = [
        pltpu.make_async_copy(
            blocks[a], wholes[a].at[:, pl.ds(pl.multiple_of(me * width, width), width)], own_sem.at[a]
        )
        for a in range(2)
    ]
    for step in range(size):
        for array in range(2):
            for piece in range(pieces):
                if step:

                    @pl.when(me >= step)
                    def _():
                        arrival(array, piece, step - 1, 1).wait_recv()

                if step < size - 1:

                    @pl.when((me >= step) & (me < size - 1))
                    def _():
                        copy(array, piece, step, 1).start()

                if step:

                    @pl.when(me + step <= size - 1)
                    def _():
                        arrival(array, piece, step - 1, -1).wait_recv()

                if step < size - 1:

                    @pl.when((me + step <= size - 1) & (me > 0))
                    def _():
                        copy(array, piece, step, -1).start()

        if step == 0:
            for mine in own:
                mine.start()
    for mine in own:
        mine.wait()
    for step in range(size - 1):
        for array in range(2):
            for piece in range(pieces):

                @pl.when((me >= step) & (me < size - 1))
                def _():
                    copy(array, piece, step, 1).wait_send()

                @pl.when((me + step <= size - 1) & (me > 0))
                def _():
                    copy(array, piece, step, -1).wait_send()


def line_gather(first, second):
    size = lax.axis_size("tensor")
    rows, width = first.shape
    pieces = 4
    sems = pltpu.SemaphoreType.DMA((2 * pieces, size - 1))
    whole = jax.ShapeDtypeStruct((rows, size * width), BF16)
    return pl.pallas_call(
        functools.partial(gather_body, size, pieces),
        in_specs=[VMEM, VMEM],
        out_specs=[VMEM, VMEM],
        out_shape=[whole, whole],
        scratch_shapes=[sems, sems, sems, sems, pltpu.SemaphoreType.DMA((2,))],
        compiler_params=pltpu.CompilerParams(
            collective_id=0, has_side_effects=True, vmem_limit_bytes=44 * 2**20
        ),
    )(first, second)


def sum_body(size, pieces, groups, *refs):
    if groups:
        terms, shares, total, summed = refs[:4]
        core_in, low, chip_in = refs[-3:]
        line, (core_sem, chip_sem, back_sem, last_sem) = refs[4:10], refs[10:14]
    else:
        terms, total = refs[:2]
        line = refs[2:8]
    up_out, up_in, down_out, down_in, line_send, line_recv = line
    me = lax.axis_index("tensor")
    rows, width = total.shape
    rows = rows // pieces
    partners = line_partners(size, me)
    if groups:
        core, chip = lax.axis_index("ctx"), lax.axis_index("dp")
        partners += [(True, {"ctx": 1 - core})]
        partners += [(True, {"dp": chip ^ bit}) for bit in range(1, groups)]
    greet(partners)

    def to_core(source, target, sem, slot):
        return pltpu.make_async_remote_copy(
            src_ref=source, dst_ref=target, send_sem=sem.at[0, slot], recv_sem=sem.at[1, slot],
            device_id={"ctx": 1 - core},
        )

    def to_chip(source, target, sem, bit):
        return pltpu.make_async_remote_copy(
            src_ref=source, dst_ref=target, send_sem=sem.at[0, bit - 1], recv_sem=sem.at[1, bit - 1],
            device_id={"dp": chip ^ bit},
        )

    def columns(owner, piece):
        at = pl.ds(pl.multiple_of(owner * width, width), width)
        return terms[pl.ds(piece * rows, rows), at]

    def line_copy(way, step, piece):
        out, into = (up_out, up_in) if way == 0 else (down_out, down_in)
        part = pl.ds(piece * rows, rows)
        slot = (way, (step - 1) * pieces + piece)
        return pltpu.make_async_remote_copy(
            src_ref=out.at[step - 1, part],
            dst_ref=into.at[step - 1, part],
            send_sem=line_send.at[slot],
            recv_sem=line_recv.at[slot],
            device_id={"tensor": me + 1 - 2 * way},
        )

    def sends(way, step):
        place = me if way == 0 else size - 1 - me
        return (place <= step - 1) & (place < size - 1)

    def line_step(step):
        reach = size - step
        for piece in range(pieces):
            part = pl.ds(piece * rows, rows)
            for way in range(2):
                out, into = (up_out, up_in) if way == 0 else (down_out, down_in)
                place = me if way == 0 else size - 1 - me
                owner = me + reach if way == 0 else me - reach

                @pl.when(sends(way, step) & (place == 0))
                def _():
                    out[step - 1, part] = columns(owner, piece)
                    line_copy(way, step, piece).start()

                if step > 1:

                    @pl.when(sends(way, step) & (place > 0))
                    def _():
                        line_copy(way, step - 1, piece).wait_recv()
                        value = columns(owner, piece).astype(F32) + into[step - 2, part].astype(F32)
                        out[step - 1, part] = value.astype(BF16)
                        line_copy(way, step, piece).start()

    orders = list(range(1, groups)) + [0] if groups else []
    for bit in orders:
        share = chip ^ bit
        to_core(shares.at[1 - core, share], core_in.at[share], core_sem, bit).start()
    line_step(1)
    for bit in orders[:-1]:
        share = chip ^ bit
        to_core(shares.at[1 - core, share], core_in.at[share], core_sem, bit).wait_recv()
        low[bit - 1] = (shares[core, share].astype(F32) + core_in[share].astype(F32)).astype(BF16)
        to_chip(low.at[bit - 1], chip_in.at[bit - 1], chip_sem, bit).start()
    for step in range(2, size):
        line_step(step)
    if groups:
        to_core(shares.at[1 - core, chip], core_in.at[chip], core_sem, 0).wait_recv()
        for bit in range(1, groups):
            to_chip(low.at[bit - 1], chip_in.at[bit - 1], chip_sem, bit).wait_recv()
        own = shares[core, chip].astype(F32) + core_in[chip].astype(F32)
        for bit in range(1, groups):
            own = own + chip_in[bit - 1].astype(F32)
        summed[core, chip] = own.astype(BF16)
        for bit in range(1, groups):
            to_chip(summed.at[core, chip], summed.at[core, chip], back_sem, bit).start()
        to_core(summed.at[core, chip], summed.at[core, chip], last_sem, 0).start()

    for piece in range(pieces):
        part = pl.ds(piece * rows, rows)
        total[part] = columns(me, piece).astype(F32)
        for way in range(2):
            into = up_in if way == 0 else down_in
            place = me if way == 0 else size - 1 - me

            @pl.when(place > 0)
            def _():
                line_copy(way, size - 1, piece).wait_recv()
                total[part] += into[size - 2, part].astype(F32)

    if groups:
        for bit in range(1, groups):
            here = summed.at[core, chip ^ bit]
            to_chip(here, here, back_sem, bit).wait_recv()
            to_core(here, here, last_sem, bit).start()
        for bit in range(groups):
            there = summed.at[1 - core, chip ^ bit]
            to_core(there, there, last_sem, bit).wait_recv()
        for bit in range(groups):
            share, here = chip ^ bit, summed.at[core, chip ^ bit]
            to_core(shares.at[1 - core, share], core_in.at[share], core_sem, bit).wait_send()
            to_core(here, here, last_sem, bit).wait_send()
            if bit:
                to_chip(low.at[bit - 1], chip_in.at[bit - 1], chip_sem, bit).wait_send()
                own_place = summed.at[core, chip]
                to_chip(own_place, own_place, back_sem, bit).wait_send()
    for step in range(1, size):
        for piece in range(pieces):
            for way in range(2):

                @pl.when(sends(way, step))
                def _():
                    line_copy(way, step, piece).wait_send()


def sums(terms, weights, number):
    size, spans, groups = lax.axis_size("tensor"), lax.axis_size("ctx"), lax.axis_size("dp")
    together = spans == 2 and groups & (groups - 1) == 0
    rows, width = terms.shape[0], terms.shape[1] // size
    pieces = 2
    passing = pltpu.VMEM((size - 1, rows, width), BF16)
    line_sems = pltpu.SemaphoreType.DMA((2, (size - 1) * pieces))
    scratch = [passing, passing, passing, passing, line_sems, line_sems]
    operands = [terms.astype(BF16)]
    shapes = [jax.ShapeDtypeStruct((rows, width), F32)]
    if together:
        joined = jnp.concatenate([w.astype(BF16) for w in weights], axis=0)
        depth, across = joined.shape
        shares = joined.reshape(spans, groups, depth // (spans * groups), across)
        operands.append(shares)
        shapes.append(jax.ShapeDtypeStruct(shares.shape, BF16))
        whole_sem = pltpu.SemaphoreType.DMA((2, groups))
        chip_sem = pltpu.SemaphoreType.DMA((2, groups - 1))
        part = shares.shape[2:]
        scratch += [
            whole_sem, chip_sem, chip_sem, whole_sem,
            pltpu.VMEM((groups, *part), BF16),
            pltpu.VMEM((groups - 1, *part), BF16),
            pltpu.VMEM((groups - 1, *part), BF16),
        ]
    results = pl.pallas_call(
        functools.partial(sum_body, size, pieces, groups if together else 0),
        in_specs=[VMEM] * len(operands),
        out_specs=[VMEM] * len(shapes),
        out_shape=shapes,
        scratch_shapes=scratch,
        compiler_params=pltpu.CompilerParams(
            collective_id=number, has_side_effects=True, vmem_limit_bytes=44 * 2**20
        ),
    )(*operands)
    if not together:
        return results[0], [lax.psum(w, ("dp", "ctx")) for w in weights]
    flat = results[1].reshape(depth, across)
    split, at = [], 0
    for w in weights:
        split.append(flat[at : at + w.shape[0]].astype(F32))
        at += w.shape[0]
    return results[0], split


def swap(block, axis, bit):
    return lax.ppermute(block, axis, [(i, i ^ bit) for i in range(lax.axis_size(axis))])


def small_sum(block, axes):
    for axis in axes:
        bit = 1
        while bit < lax.axis_size(axis):
            block = block + swap(block, axis, bit)
            bit *= 2
    return block


def attention_body(
    heads, chunk, qmax, kmin, q, g, k, v, qpos, kpos, att, dq, dk, dv, e_keep, mass, out, k_head, v_head
):
    block = pl.program_id(1)
    width = q.shape[-1]
    chunks = k.shape[1] // chunk
    lane = lax.broadcasted_iota(jnp.int32, (1, width), 1)
    picks = [((lane >= h * HEAD) & (lane < (h + 1) * HEAD)).astype(F32) for h in range(heads)]

    @pl.when(block == 0)
    def _():
        dk[...] = jnp.zeros_like(dk)
        dv[...] = jnp.zeros_like(dv)
        for h in range(heads):
            k_head[h] = k[0] * picks[h].astype(BF16)
            v_head[h] = v[0] * picks[h].astype(BF16)

    nt = (((1,), (1,)), ((), ()))
    tn = (((0,), (0,)), ((), ()))
    dq[...] = jnp.zeros_like(dq)
    queries = q[0]
    grads = g[0]
    result = jnp.zeros(grads.shape, F32)
    for h in range(heads):
        mass[...] = jnp.zeros_like(mass)
        out[...] = jnp.zeros_like(out)
        for c in range(chunks):
            part = pl.ds(c * chunk, chunk)

            @pl.when(kmin[c] <= qmax[block])
            def _():
                raw = lax.dot_general(queries, k_head[h, part], nt, preferred_element_type=F32)
                e = jnp.where(kpos[:, part] <= qpos[...], jnp.exp(raw), 0.0)
                e_keep[:, part] = e
                mass[...] += jnp.sum(e, axis=1, keepdims=True)
                out[...] += jnp.dot(e.astype(BF16), v_head[h, part], preferred_element_type=F32)

        inverse = 1.0 / mass[...]
        attended = out[...] * inverse
        result = result + attended
        scaled = (grads * inverse).astype(BF16)
        corr = jnp.sum(grads * attended, axis=1, keepdims=True) * inverse
        pick = picks[h].astype(BF16)
        scaled_head = scaled * pick
        q_head = queries * pick
        for c in range(chunks):
            part = pl.ds(c * chunk, chunk)

            @pl.when(kmin[c] <= qmax[block])
            def _():
                e = e_keep[:, part]
                slope = lax.dot_general(scaled, v_head[h, part], nt, preferred_element_type=F32)
                d_raw = (e * (slope - corr)).astype(BF16)
                dq[0] += jnp.dot(d_raw, k_head[h, part], preferred_element_type=F32)
                dk[0, part] += lax.dot_general(d_raw, q_head, tn, preferred_element_type=F32)
                dv[0, part] += lax.dot_general(
                    e.astype(BF16), scaled_head, tn, preferred_element_type=F32
                )

    att[0] = result.astype(BF16)


def attention(q, g, k, v, qpos, kpos):
    seqs, q_rows, width = q.shape
    k_rows = k.shape[1]
    heads = width // HEAD
    block, chunk = min(512, q_rows), min(512, k_rows)
    qmax = jnp.max(qpos.reshape(-1, block), axis=1)
    kmin = jnp.min(kpos.reshape(-1, chunk), axis=1)
    by_block = pl.BlockSpec((1, block, width), lambda s, b: (s, b, 0))
    by_seq = pl.BlockSpec((1, k_rows, width), lambda s, b: (s, 0, 0))
    smem = pl.BlockSpec(memory_space=pltpu.SMEM)
    pairs = seqs * q_rows * k_rows * width
    return pl.pallas_call(
        functools.partial(attention_body, heads, chunk),
        grid=(seqs, q_rows // block),
        in_specs=[
            smem,
            smem,
            by_block,
            by_block,
            by_seq,
            by_seq,
            pl.BlockSpec((block, 1), lambda s, b: (b, 0)),
            pl.BlockSpec((1, k_rows), lambda s, b: (0, 0)),
        ],
        out_specs=[by_block, by_block, by_seq, by_seq],
        out_shape=[
            jax.ShapeDtypeStruct(q.shape, BF16),
            jax.ShapeDtypeStruct(q.shape, F32),
            jax.ShapeDtypeStruct(k.shape, F32),
            jax.ShapeDtypeStruct(k.shape, F32),
        ],
        scratch_shapes=[
            pltpu.VMEM((block, k_rows), F32),
            pltpu.VMEM((block, 1), F32),
            pltpu.VMEM((block, width), F32),
            pltpu.VMEM((heads, k_rows, width), BF16),
            pltpu.VMEM((heads, k_rows, width), BF16),
        ],
        cost_estimate=pl.CostEstimate(
            flops=48 * pairs, bytes_accessed=16 * seqs * k_rows * width, transcendentals=pairs // HEAD
        ),
        compiler_params=pltpu.CompilerParams(vmem_limit_bytes=44 * 2**20),
    )(qmax, kmin, q, g, k, v, qpos[:, None], kpos[None, :])


def norm_forward(full_rows):
    average = jnp.mean(full_rows, axis=-1, keepdims=True)
    centred = full_rows - average
    variance = jnp.mean(centred * centred, axis=-1, keepdims=True)
    inverse_scale = lax.rsqrt(variance + 1e-05)
    return (centred * inverse_scale, inverse_scale)


def rotation_tables(positions, width):
    half_rot = ROT // 2
    dim = jnp.arange(width, dtype=jnp.int32) % HEAD
    frequency = 10000.0 ** (-2.0 * (dim % half_rot).astype(F32) / ROT)
    angle = positions.astype(F32)[:, None] * frequency[None, :]
    cosine = jnp.where(dim < ROT, jnp.cos(angle), 1.0)
    sine = jnp.sin(angle)
    lower = jnp.where(dim < half_rot, sine, 0.0)
    upper = jnp.where((dim >= half_rot) & (dim < ROT), sine, 0.0)
    return lax.optimization_barrier((cosine, lower, upper))


def rotate(field, tables, sign):
    cosine, lower, upper = tables
    half_rot = ROT // 2
    return (
        field * cosine
        - sign * jnp.roll(field, -half_rot, axis=1) * lower
        + sign * jnp.roll(field, half_rot, axis=1) * upper
    )


def local(
    tokens,
    span_of_slot,
    norm_gain,
    norm_bias,
    qkv_weight,
    qkv_bias,
    attn_out_weight,
    out_bias,
    mlp_in_weight,
    mlp_in_bias,
    mlp_out_weight,
    cotangent,
):
    tok_rows, local_width = tokens.shape
    ctx_count = lax.axis_size("ctx")
    span_len = LEN // (2 * ctx_count)
    seq_count = tok_rows // (2 * span_len)
    seq_rows = 2 * span_len
    head_width = qkv_weight.shape[2]
    column_start = lax.axis_index("tensor") * local_width

    full_tokens, full_grads = line_gather(tokens, cotangent)

    slot_table = span_of_slot.reshape(ctx_count, 2)
    offsets = jnp.arange(span_len, dtype=jnp.int32)

    def positions_of(spans):
        return (spans[..., None] * span_len + offsets).reshape(-1)

    own_spans = lax.dynamic_index_in_dim(slot_table, lax.axis_index("ctx"), 0, False)
    query_pos = positions_of(own_spans)
    tables = rotation_tables(jnp.tile(query_pos, seq_count), head_width)

    normed, inverse_scale = norm_forward(full_tokens.astype(F32))
    gains = norm_gain.astype(F32)
    shifts = norm_bias.astype(F32)
    norm_first = (normed * gains[0] + shifts[0]).astype(BF16)
    norm_second = (normed * gains[1] + shifts[1]).astype(BF16)

    projected = [
        jnp.dot(norm_first, qkv_weight[c], preferred_element_type=F32) + qkv_bias[c].astype(F32)
        for c in range(3)
    ]
    query_b = (rotate(projected[0], tables, 1.0).astype(BF16) * BF16(0.125)).reshape(
        seq_count, seq_rows, head_width
    )
    key_value = jnp.stack([rotate(projected[1], tables, 1.0).astype(BF16), projected[2].astype(BF16)])
    if ctx_count == 2:
        other_spans = lax.dynamic_index_in_dim(slot_table, 1 - lax.axis_index("ctx"), 0, False)
        key_pos = positions_of(jnp.concatenate([own_spans, other_spans]))
        shards = [key_value, swap(key_value, "ctx", 1)]
    else:
        key_pos = positions_of(span_of_slot)
        shards = list(lax.all_gather(key_value, "ctx"))
    key_value = jnp.concatenate(
        [shard.reshape(2, seq_count, seq_rows, head_width) for shard in shards], axis=2
    )

    hidden = jnp.dot(norm_second, mlp_in_weight, preferred_element_type=F32) + mlp_in_bias.astype(F32)
    normal_cdf = 0.5 * (1.0 + lax.erf(hidden * 0.7071067811865476))
    density = jnp.exp(-0.5 * hidden * hidden) * 0.3989422804014327
    activated_b, gelu_slope = lax.optimization_barrier(
        ((hidden * normal_cdf).astype(BF16), normal_cdf + hidden * density)
    )

    grad_local = cotangent.astype(F32)
    mlp_out_term = jnp.dot(activated_b.T, full_grads, preferred_element_type=F32)
    grad_activated = jnp.dot(full_grads, mlp_out_weight.T, preferred_element_type=F32)
    grad_hidden = lax.optimization_barrier((grad_activated * gelu_slope).astype(BF16))
    mlp_in_term = jnp.dot(norm_second.T, grad_hidden, preferred_element_type=F32)

    grad_attended = jnp.dot(full_grads, attn_out_weight.T, preferred_element_type=F32)
    attended_b, grad_query, grad_key, grad_value = attention(
        query_b,
        grad_attended.reshape(seq_count, seq_rows, head_width),
        key_value[0],
        key_value[1],
        query_pos,
        key_pos,
    )
    attended_b = attended_b.reshape(tok_rows, head_width)

    if ctx_count == 2:

        def to_owner(grad):
            return (grad[:, :seq_rows] + swap(grad[:, seq_rows:], "ctx", 1)).reshape(
                tok_rows, head_width
            )
    else:

        def to_owner(grad):
            shares = grad.reshape(seq_count, ctx_count, seq_rows, head_width).swapaxes(0, 1)
            return lax.psum_scatter(
                shares.reshape(ctx_count * tok_rows, head_width), "ctx", scatter_dimension=0, tiled=True
            )

    attn_out_term = jnp.dot(attended_b.T, full_grads, preferred_element_type=F32)
    branch_terms = jnp.dot(attended_b, attn_out_weight, preferred_element_type=F32) + jnp.dot(
        activated_b, mlp_out_weight, preferred_element_type=F32
    )
    half = mlp_in_term.shape[0] // 2
    branch_sum, (mlp_out_grad, mlp_in_first) = sums(branch_terms, [mlp_out_term, mlp_in_term[:half]], 1)
    bias_rows = out_bias.astype(F32)
    mixed = (tokens.astype(F32) + branch_sum + bias_rows[0] + bias_rows[1]).astype(BF16)

    second_part = jnp.dot(grad_hidden, mlp_in_weight.T, preferred_element_type=F32)
    grad_proj = [
        rotate(0.125 * grad_query.reshape(tok_rows, head_width), tables, -1.0).astype(BF16),
        rotate(to_owner(grad_key), tables, -1.0).astype(BF16),
        to_owner(grad_value).astype(BF16),
    ]
    grad_proj = lax.optimization_barrier(jnp.concatenate(grad_proj, axis=1))
    qkv_term = jnp.dot(grad_proj.T, norm_first, preferred_element_type=F32)
    flat_weight = qkv_weight.transpose(1, 0, 2).reshape(qkv_weight.shape[1], 3 * head_width)
    first_part = jnp.dot(grad_proj, flat_weight.T, preferred_element_type=F32)

    combined = first_part * gains[0] + second_part * gains[1]
    back_sum, (mlp_in_second, attn_out_grad, qkv_grad) = sums(
        combined, [mlp_in_term[half:], attn_out_term, qkv_term], 2
    )
    mlp_in_grad = jnp.concatenate([mlp_in_first, mlp_in_second], axis=0)
    means = small_sum(
        jnp.stack([jnp.sum(combined, axis=1), jnp.sum(combined * normed, axis=1)]), ("tensor",)
    ) * (1.0 / full_tokens.shape[1])
    own_normed = lax.dynamic_slice_in_dim(normed, column_start, local_width, 1)
    input_grad = grad_local + inverse_scale * (
        back_sum - means[0][:, None] - own_normed * means[1][:, None]
    )

    norm_term = jnp.stack(
        [
            jnp.sum(first_part * normed, axis=0),
            jnp.sum(second_part * normed, axis=0),
            jnp.sum(first_part, axis=0),
            jnp.sum(second_part, axis=0),
        ]
    )
    norm_sum = lax.dynamic_slice_in_dim(
        small_sum(norm_term, ("tensor", "ctx", "dp")), column_start, local_width, 1
    )
    bias_sum = small_sum(
        jnp.concatenate(
            [
                jnp.sum(grad_proj.astype(F32), axis=0),
                jnp.sum(grad_local, axis=0),
                jnp.sum(grad_hidden.astype(F32), axis=0),
            ]
        ),
        ("ctx", "dp"),
    )
    out_bias_grad = bias_sum[3 * head_width : 3 * head_width + local_width]
    return (
        mixed,
        input_grad,
        norm_sum[0:2],
        norm_sum[2:4],
        qkv_grad.reshape(3, head_width, -1).transpose(0, 2, 1),
        bias_sum[: 3 * head_width].reshape(3, head_width),
        attn_out_grad,
        jnp.stack([out_bias_grad, out_bias_grad]),
        mlp_in_grad,
        bias_sum[3 * head_width + local_width :],
        mlp_out_grad,
    )


def solution(mesh):
    placed = (
        P(("dp", "ctx"), "tensor"),
        P(),
        P(),
        P(),
        P(None, None, "tensor"),
        P(None, "tensor"),
        P("tensor", None),
        P(None, "tensor"),
        P(None, "tensor"),
        P("tensor"),
        P("tensor", None),
        P(("dp", "ctx"), "tensor"),
    )
    return jax.shard_map(
        local,
        mesh=mesh,
        in_specs=placed,
        out_specs=(
            P(("dp", "ctx"), "tensor"),
            P(("dp", "ctx"), "tensor"),
            P(None, "tensor"),
            P(None, "tensor"),
            P(None, None, "tensor"),
            P(None, "tensor"),
            P("tensor", None),
            P(None, "tensor"),
            P(None, "tensor"),
            P("tensor"),
            P("tensor", None),
        ),
        check_vma=False,
    )
```

```python
import functools

import jax
import jax.numpy as jnp
from jax import lax
from jax.experimental import pallas as pl
from jax.experimental.pallas import tpu as pltpu
from jax.sharding import PartitionSpec as P

HEAD = 64
ROT = 16
LEN = 2048
BF16 = jnp.bfloat16
F32 = jnp.float32


VMEM = pl.BlockSpec(memory_space=pltpu.VMEM)


def greet(partners):
    barrier = pltpu.get_barrier_semaphore()
    expected = 0
    for exists, device in partners:
        if exists is True:
            pl.semaphore_signal(barrier, inc=1, device_id=device)
            expected = expected + 1
        else:

            @pl.when(exists)
            def _():
                pl.semaphore_signal(barrier, inc=1, device_id=device)

            expected = expected + exists.astype(jnp.int32)
    pl.semaphore_wait(barrier, expected)


def line_partners(size, me):
    return [(me > 0, {"tensor": me - 1}), (me < size - 1, {"tensor": me + 1})]


def gather_body(size, pieces, *refs):
    arrays = (len(refs) - 5) // 2
    blocks, wholes = refs[:arrays], refs[arrays : 2 * arrays]
    up_send, up_recv, down_send, down_recv, own_sem = refs[2 * arrays :]
    me = lax.axis_index("tensor")
    rows, width = blocks[0].shape
    rows = rows // pieces
    greet(line_partners(size, me))

    def place(array, owner, piece):
        columns = pl.ds(pl.multiple_of(owner * width, width), width)
        return wholes[array].at[pl.ds(piece * rows, rows), columns]

    def copy(array, piece, step, sign):
        slot = (array * pieces + piece, step)
        send, recv = (up_send, up_recv) if sign > 0 else (down_send, down_recv)
        target = place(array, me - sign * step, piece)
        source = blocks[array].at[pl.ds(piece * rows, rows)] if step == 0 else target
        return pltpu.make_async_remote_copy(
            src_ref=source,
            dst_ref=target,
            send_sem=send.at[slot],
            recv_sem=recv.at[slot],
            device_id={"tensor": me + sign},
        )

    def arrival(array, piece, step, sign):
        slot = (array * pieces + piece, step)
        send, recv = (up_send, up_recv) if sign > 0 else (down_send, down_recv)
        target = place(array, me - sign * (step + 1), piece)
        return pltpu.make_async_remote_copy(
            src_ref=target,
            dst_ref=target,
            send_sem=send.at[slot],
            recv_sem=recv.at[slot],
            device_id={"tensor": me - sign},
        )

    own = [
        pltpu.make_async_copy(
            blocks[a], wholes[a].at[:, pl.ds(pl.multiple_of(me * width, width), width)], own_sem.at[a]
        )
        for a in range(arrays)
    ]
    for step in range(size):
        for array in range(arrays):
            for piece in range(pieces):
                if step:

                    @pl.when(me >= step)
                    def _():
                        arrival(array, piece, step - 1, 1).wait_recv()

                if step < size - 1:

                    @pl.when((me >= step) & (me < size - 1))
                    def _():
                        copy(array, piece, step, 1).start()

                if step:

                    @pl.when(me + step <= size - 1)
                    def _():
                        arrival(array, piece, step - 1, -1).wait_recv()

                if step < size - 1:

                    @pl.when((me + step <= size - 1) & (me > 0))
                    def _():
                        copy(array, piece, step, -1).start()

        if step == 0:
            for mine in own:
                mine.start()
    for mine in own:
        mine.wait()
    for step in range(size - 1):
        for array in range(arrays):
            for piece in range(pieces):

                @pl.when((me >= step) & (me < size - 1))
                def _():
                    copy(array, piece, step, 1).wait_send()

                @pl.when((me + step <= size - 1) & (me > 0))
                def _():
                    copy(array, piece, step, -1).wait_send()


def line_gather(*blocks):
    size, count = lax.axis_size("tensor"), len(blocks)
    rows, width = blocks[0].shape
    pieces = 4
    sems = pltpu.SemaphoreType.DMA((count * pieces, size - 1))
    whole = jax.ShapeDtypeStruct((rows, size * width), BF16)
    return pl.pallas_call(
        functools.partial(gather_body, size, pieces),
        in_specs=[VMEM] * count,
        out_specs=[VMEM] * count,
        out_shape=[whole] * count,
        scratch_shapes=[sems, sems, sems, sems, pltpu.SemaphoreType.DMA((count,))],
        compiler_params=pltpu.CompilerParams(
            collective_id=0, has_side_effects=True, vmem_limit_bytes=12 * 2**20
        ),
    )(*blocks)


def sum_body(size, pieces, groups, small_steps, *refs):
    if small_steps:
        small_in, small_out, refs = refs[0], refs[1], refs[2:]
        small_sum, small_land, small_sem, refs = refs[-3], refs[-2], refs[-1], refs[:-3]
    if groups:
        terms, shares, total, summed = refs[:4]
        core_in, low, chip_in = refs[-3:]
        line, (core_sem, chip_sem, back_sem, last_sem) = refs[4:10], refs[10:14]
    else:
        terms, total = refs[:2]
        line = refs[2:8]
    up_out, up_in, down_out, down_in, line_send, line_recv = line
    me = lax.axis_index("tensor")
    rows, width = total.shape
    rows = rows // pieces
    core, chip = lax.axis_index("ctx"), lax.axis_index("dp")
    partners = [(True, {"tensor": lax.rem(me + k, size)}) for k in range(1, size)]
    if groups:
        partners += [(True, {"ctx": 1 - core})]
        partners += [(True, {"dp": chip ^ bit}) for bit in range(1, groups)]
    elif small_steps:
        partners += [
            (True, {axis: lax.axis_index(axis) ^ bit}) for axis, bit in small_steps if axis != "tensor"
        ]
    greet(partners)

    def small_copy(step):
        axis, bit = small_steps[step]
        return pltpu.make_async_remote_copy(
            src_ref=small_sum.at[step], dst_ref=small_land.at[step],
            send_sem=small_sem.at[0, step], recv_sem=small_sem.at[1, step],
            device_id={axis: lax.axis_index(axis) ^ bit},
        )

    waiting = list(range(len(small_steps)))

    def small_next():
        if not waiting:
            return
        step = waiting.pop(0)
        small_copy(step).wait_recv()
        row = lax.broadcasted_iota(jnp.int32, small_in.shape, 0)
        counts = (row < 4) | (row >= 6) if small_steps[step][0] == "tensor" else row < 6
        small_sum[step + 1] = small_sum[step] + jnp.where(counts, small_land[step], 0.0)
        if waiting:
            small_copy(step + 1).start()
        else:
            small_out[...] = small_sum[step + 1]

    if small_steps:
        small_sum[0] = small_in[...]
        small_copy(0).start()

    def to_core(source, target, sem, slot):
        return pltpu.make_async_remote_copy(
            src_ref=source, dst_ref=target, send_sem=sem.at[0, slot], recv_sem=sem.at[1, slot],
            device_id={"ctx": 1 - core},
        )

    def to_chip(source, target, sem, bit):
        return pltpu.make_async_remote_copy(
            src_ref=source, dst_ref=target, send_sem=sem.at[0, bit - 1], recv_sem=sem.at[1, bit - 1],
            device_id={"dp": chip ^ bit},
        )

    def columns(owner, piece):
        at = pl.ds(pl.multiple_of(owner * width, width), width)
        return terms[pl.ds(piece * rows, rows), at]

    def line_copy(way, step, piece):
        out, into = (up_out, up_in) if way == 0 else (down_out, down_in)
        part = pl.ds(piece * rows, rows)
        slot = (way, (step - 1) * pieces + piece)
        return pltpu.make_async_remote_copy(
            src_ref=out.at[step - 1, part],
            dst_ref=into.at[step - 1, part],
            send_sem=line_send.at[slot],
            recv_sem=line_recv.at[slot],
            device_id={"tensor": me + 1 - 2 * way},
        )

    def sends(way, step):
        place = me if way == 0 else size - 1 - me
        return (place <= step - 1) & (place < size - 1)

    def line_step(step):
        reach = size - step
        for piece in range(pieces):
            part = pl.ds(piece * rows, rows)
            for way in range(2):
                out, into = (up_out, up_in) if way == 0 else (down_out, down_in)
                place = me if way == 0 else size - 1 - me
                owner = me + reach if way == 0 else me - reach

                @pl.when(sends(way, step) & (place == 0))
                def _():
                    out[step - 1, part] = columns(owner, piece)
                    line_copy(way, step, piece).start()

                if step > 1:

                    @pl.when(sends(way, step) & (place > 0))
                    def _():
                        line_copy(way, step - 1, piece).wait_recv()
                        value = columns(owner, piece).astype(F32) + into[step - 2, part].astype(F32)
                        out[step - 1, part] = value.astype(BF16)
                        line_copy(way, step, piece).start()

    orders = list(range(1, groups)) + [0] if groups else []
    for bit in orders:
        share = chip ^ bit
        to_core(shares.at[1 - core, share], core_in.at[share], core_sem, bit).start()
    line_step(1)
    for bit in orders[:-1]:
        share = chip ^ bit
        to_core(shares.at[1 - core, share], core_in.at[share], core_sem, bit).wait_recv()
        low[bit - 1] = (shares[core, share].astype(F32) + core_in[share].astype(F32)).astype(BF16)
        to_chip(low.at[bit - 1], chip_in.at[bit - 1], chip_sem, bit).start()
        small_next()
    for step in range(2, size):
        line_step(step)
        small_next()
    while waiting:
        small_next()
    if groups:
        to_core(shares.at[1 - core, chip], core_in.at[chip], core_sem, 0).wait_recv()
        for bit in range(1, groups):
            to_chip(low.at[bit - 1], chip_in.at[bit - 1], chip_sem, bit).wait_recv()
        own = shares[core, chip].astype(F32) + core_in[chip].astype(F32)
        for bit in range(1, groups):
            own = own + chip_in[bit - 1].astype(F32)
        summed[core, chip] = own.astype(BF16)
        for bit in range(1, groups):
            to_chip(summed.at[core, chip], summed.at[core, chip], back_sem, bit).start()
        to_core(summed.at[core, chip], summed.at[core, chip], last_sem, 0).start()

    for piece in range(pieces):
        part = pl.ds(piece * rows, rows)
        total[part] = columns(me, piece).astype(F32)
        for way in range(2):
            into = up_in if way == 0 else down_in
            place = me if way == 0 else size - 1 - me

            @pl.when(place > 0)
            def _():
                line_copy(way, size - 1, piece).wait_recv()
                total[part] += into[size - 2, part].astype(F32)

    if groups:
        for bit in range(1, groups):
            here = summed.at[core, chip ^ bit]
            to_chip(here, here, back_sem, bit).wait_recv()
            to_core(here, here, last_sem, bit).start()
        for bit in range(groups):
            there = summed.at[1 - core, chip ^ bit]
            to_core(there, there, last_sem, bit).wait_recv()
        for bit in range(groups):
            share, here = chip ^ bit, summed.at[core, chip ^ bit]
            to_core(shares.at[1 - core, share], core_in.at[share], core_sem, bit).wait_send()
            to_core(here, here, last_sem, bit).wait_send()
            if bit:
                to_chip(low.at[bit - 1], chip_in.at[bit - 1], chip_sem, bit).wait_send()
                own_place = summed.at[core, chip]
                to_chip(own_place, own_place, back_sem, bit).wait_send()
    for step in range(len(small_steps)):
        small_copy(step).wait_send()
    for step in range(1, size):
        for piece in range(pieces):
            for way in range(2):

                @pl.when(sends(way, step))
                def _():
                    line_copy(way, step, piece).wait_send()


def sums(terms, weights, number, small=None):
    size, spans, groups = lax.axis_size("tensor"), lax.axis_size("ctx"), lax.axis_size("dp")
    together = spans == 2 and groups & (groups - 1) == 0
    rows, width = terms.shape[0], terms.shape[1] // size
    pieces = 2
    passing = pltpu.VMEM((size - 1, rows, width), BF16)
    line_sems = pltpu.SemaphoreType.DMA((2, (size - 1) * pieces))
    scratch = [passing, passing, passing, passing, line_sems, line_sems]
    operands = [terms.astype(BF16)]
    shapes = [jax.ShapeDtypeStruct((rows, width), F32)]
    if together:
        joined = jnp.concatenate([w.astype(BF16) for w in weights], axis=0)
        depth, across = joined.shape
        shares = joined.reshape(spans, groups, depth // (spans * groups), across)
        operands.append(shares)
        shapes.append(jax.ShapeDtypeStruct(shares.shape, BF16))
        whole_sem = pltpu.SemaphoreType.DMA((2, groups))
        chip_sem = pltpu.SemaphoreType.DMA((2, groups - 1))
        part = shares.shape[2:]
        scratch += [
            whole_sem, chip_sem, chip_sem, whole_sem,
            pltpu.VMEM((groups, *part), BF16),
            pltpu.VMEM((groups - 1, *part), BF16),
            pltpu.VMEM((groups - 1, *part), BF16),
        ]
    small_steps = []
    if small is not None:
        for axis in ("tensor", "ctx", "dp"):
            bit = 1
            while bit < lax.axis_size(axis):
                small_steps.append((axis, bit))
                bit *= 2
        count = len(small_steps)
        operands = [small] + operands
        shapes = [jax.ShapeDtypeStruct(small.shape, F32)] + shapes
        scratch += [
            pltpu.VMEM((count + 1, *small.shape), F32),
            pltpu.VMEM((count, *small.shape), F32),
            pltpu.SemaphoreType.DMA((2, count)),
        ]
    body = functools.partial(sum_body, size, pieces, groups if together else 0, small_steps)
    if small is not None:
        plain, ins = body, len(operands)

        def body(*refs):
            plain(refs[0], refs[ins], *refs[1:ins], *refs[ins + 1 :])

    results = pl.pallas_call(
        body,
        in_specs=[VMEM] * len(operands),
        out_specs=[VMEM] * len(shapes),
        out_shape=shapes,
        scratch_shapes=scratch,
        compiler_params=pltpu.CompilerParams(
            collective_id=number, has_side_effects=True, vmem_limit_bytes=28 * 2**20
        ),
    )(*operands)
    shared = None
    if small is not None:
        shared, results = results[0], results[1:]
    if not together:
        return results[0], [lax.psum(w, ("dp", "ctx")) for w in weights], shared
    flat = results[1].reshape(depth, across)
    split, at = [], 0
    for w in weights:
        split.append(flat[at : at + w.shape[0]].astype(F32))
        at += w.shape[0]
    return results[0], split, shared


def swap(block, axis, bit):
    return lax.ppermute(block, axis, [(i, i ^ bit) for i in range(lax.axis_size(axis))])


def attention_body(
    heads, chunk, qmax, kmin, q, g, k, v, qpos, kpos, att, dq, dk, dv, e_keep, mass, out, k_head, v_head
):
    block = pl.program_id(1)
    width = q.shape[-1]
    chunks = k.shape[1] // chunk
    lane = lax.broadcasted_iota(jnp.int32, (1, width), 1)
    picks = [((lane >= h * HEAD) & (lane < (h + 1) * HEAD)).astype(F32) for h in range(heads)]

    @pl.when(block == 0)
    def _():
        dk[...] = jnp.zeros_like(dk)
        dv[...] = jnp.zeros_like(dv)
        for h in range(heads):
            k_head[h] = k[0] * picks[h].astype(BF16)
            v_head[h] = v[0] * picks[h].astype(BF16)

    nt = (((1,), (1,)), ((), ()))
    tn = (((0,), (0,)), ((), ()))
    dq[...] = jnp.zeros_like(dq)
    queries = q[0]
    grads = g[0]
    result = jnp.zeros(grads.shape, F32)
    for h in range(heads):
        mass[...] = jnp.zeros_like(mass)
        out[...] = jnp.zeros_like(out)
        for c in range(chunks):
            part = pl.ds(c * chunk, chunk)

            @pl.when(kmin[c] <= qmax[block])
            def _():
                raw = lax.dot_general(queries, k_head[h, part], nt, preferred_element_type=F32)
                e = jnp.where(kpos[:, part] <= qpos[...], jnp.exp(raw), 0.0)
                e_keep[:, part] = e
                mass[...] += jnp.sum(e, axis=1, keepdims=True)
                out[...] += jnp.dot(e.astype(BF16), v_head[h, part], preferred_element_type=F32)

        inverse = 1.0 / mass[...]
        attended = out[...] * inverse
        result = result + attended
        scaled = (grads * inverse).astype(BF16)
        corr = jnp.sum(grads * attended, axis=1, keepdims=True) * inverse
        pick = picks[h].astype(BF16)
        scaled_head = scaled * pick
        q_head = queries * pick
        for c in range(chunks):
            part = pl.ds(c * chunk, chunk)

            @pl.when(kmin[c] <= qmax[block])
            def _():
                e = e_keep[:, part]
                slope = lax.dot_general(scaled, v_head[h, part], nt, preferred_element_type=F32)
                d_raw = (e * (slope - corr)).astype(BF16)
                dq[0] += jnp.dot(d_raw, k_head[h, part], preferred_element_type=F32)
                dk[0, part] += lax.dot_general(d_raw, q_head, tn, preferred_element_type=F32)
                dv[0, part] += lax.dot_general(
                    e.astype(BF16), scaled_head, tn, preferred_element_type=F32
                )

    att[0] = result.astype(BF16)


def attention(q, g, k, v, qpos, kpos):
    seqs, q_rows, width = q.shape
    k_rows = k.shape[1]
    heads = width // HEAD
    block, chunk = min(512, q_rows), min(512, k_rows)
    qmax = jnp.max(qpos.reshape(-1, block), axis=1)
    kmin = jnp.min(kpos.reshape(-1, chunk), axis=1)
    by_block = pl.BlockSpec((1, block, width), lambda s, b: (s, b, 0))
    by_seq = pl.BlockSpec((1, k_rows, width), lambda s, b: (s, 0, 0))
    smem = pl.BlockSpec(memory_space=pltpu.SMEM)
    pairs = seqs * q_rows * k_rows * width
    return pl.pallas_call(
        functools.partial(attention_body, heads, chunk),
        grid=(seqs, q_rows // block),
        in_specs=[
            smem,
            smem,
            by_block,
            by_block,
            by_seq,
            by_seq,
            pl.BlockSpec((block, 1), lambda s, b: (b, 0)),
            pl.BlockSpec((1, k_rows), lambda s, b: (0, 0)),
        ],
        out_specs=[by_block, by_block, by_seq, by_seq],
        out_shape=[
            jax.ShapeDtypeStruct(q.shape, BF16),
            jax.ShapeDtypeStruct(q.shape, F32),
            jax.ShapeDtypeStruct(k.shape, F32),
            jax.ShapeDtypeStruct(k.shape, F32),
        ],
        scratch_shapes=[
            pltpu.VMEM((block, k_rows), F32),
            pltpu.VMEM((block, 1), F32),
            pltpu.VMEM((block, width), F32),
            pltpu.VMEM((heads, k_rows, width), BF16),
            pltpu.VMEM((heads, k_rows, width), BF16),
        ],
        cost_estimate=pl.CostEstimate(
            flops=48 * pairs, bytes_accessed=16 * seqs * k_rows * width, transcendentals=pairs // HEAD
        ),
        compiler_params=pltpu.CompilerParams(vmem_limit_bytes=38 * 2**20),
    )(qmax, kmin, q, g, k, v, qpos[:, None], kpos[None, :])


def norm_forward(full_rows):
    average = jnp.mean(full_rows, axis=-1, keepdims=True)
    centred = full_rows - average
    variance = jnp.mean(centred * centred, axis=-1, keepdims=True)
    inverse_scale = lax.rsqrt(variance + 1e-05)
    return (centred * inverse_scale, inverse_scale)


def rotation_tables(positions, width):
    half_rot = ROT // 2
    dim = jnp.arange(width, dtype=jnp.int32) % HEAD
    frequency = 10000.0 ** (-2.0 * (dim % half_rot).astype(F32) / ROT)
    angle = positions.astype(F32)[:, None] * frequency[None, :]
    cosine = jnp.where(dim < ROT, jnp.cos(angle), 1.0)
    sine = jnp.sin(angle)
    lower = jnp.where(dim < half_rot, sine, 0.0)
    upper = jnp.where((dim >= half_rot) & (dim < ROT), sine, 0.0)
    return lax.optimization_barrier((cosine, lower, upper))


def rotate(field, tables, sign):
    cosine, lower, upper = tables
    half_rot = ROT // 2
    return (
        field * cosine
        - sign * jnp.roll(field, -half_rot, axis=1) * lower
        + sign * jnp.roll(field, half_rot, axis=1) * upper
    )


def local(
    tokens,
    span_of_slot,
    norm_gain,
    norm_bias,
    qkv_weight,
    qkv_bias,
    attn_out_weight,
    out_bias,
    mlp_in_weight,
    mlp_in_bias,
    mlp_out_weight,
    cotangent,
):
    tok_rows, local_width = tokens.shape
    ctx_count = lax.axis_size("ctx")
    span_len = LEN // (2 * ctx_count)
    seq_count = tok_rows // (2 * span_len)
    seq_rows = 2 * span_len
    head_width = qkv_weight.shape[2]
    column_start = lax.axis_index("tensor") * local_width

    (full_tokens,) = line_gather(tokens)
    full_tokens, late_cotangent = lax.optimization_barrier((full_tokens, cotangent))
    full_grads = lax.all_gather(late_cotangent, "tensor", axis=1, tiled=True)

    slot_table = span_of_slot.reshape(ctx_count, 2)
    offsets = jnp.arange(span_len, dtype=jnp.int32)

    def positions_of(spans):
        return (spans[..., None] * span_len + offsets).reshape(-1)

    own_spans = lax.dynamic_index_in_dim(slot_table, lax.axis_index("ctx"), 0, False)
    query_pos = positions_of(own_spans)
    tables = rotation_tables(jnp.tile(query_pos, seq_count), head_width)

    normed, inverse_scale = norm_forward(full_tokens.astype(F32))
    gains = norm_gain.astype(F32)
    shifts = norm_bias.astype(F32)
    norm_first = (normed * gains[0] + shifts[0]).astype(BF16)
    norm_second = (normed * gains[1] + shifts[1]).astype(BF16)

    projected = [
        jnp.dot(norm_first, qkv_weight[c], preferred_element_type=F32) + qkv_bias[c].astype(F32)
        for c in range(3)
    ]
    query_b = (rotate(projected[0], tables, 1.0).astype(BF16) * BF16(0.125)).reshape(
        seq_count, seq_rows, head_width
    )
    key_value = jnp.stack([rotate(projected[1], tables, 1.0).astype(BF16), projected[2].astype(BF16)])
    if ctx_count == 2:
        other_spans = lax.dynamic_index_in_dim(slot_table, 1 - lax.axis_index("ctx"), 0, False)
        key_pos = positions_of(jnp.concatenate([own_spans, other_spans]))
        shards = [key_value, swap(key_value, "ctx", 1)]
    else:
        key_pos = positions_of(span_of_slot)
        shards = list(lax.all_gather(key_value, "ctx"))
    key_value = jnp.concatenate(
        [shard.reshape(2, seq_count, seq_rows, head_width) for shard in shards], axis=2
    )

    hidden = jnp.dot(norm_second, mlp_in_weight, preferred_element_type=F32) + mlp_in_bias.astype(F32)
    normal_cdf = 0.5 * (1.0 + lax.erf(hidden * 0.7071067811865476))
    density = jnp.exp(-0.5 * hidden * hidden) * 0.3989422804014327
    activated_b, gelu_slope = lax.optimization_barrier(
        ((hidden * normal_cdf).astype(BF16), normal_cdf + hidden * density)
    )

    grad_local = cotangent.astype(F32)
    mlp_out_term = jnp.dot(activated_b.T, full_grads, preferred_element_type=F32)
    grad_activated = jnp.dot(full_grads, mlp_out_weight.T, preferred_element_type=F32)
    grad_hidden = lax.optimization_barrier((grad_activated * gelu_slope).astype(BF16))
    mlp_in_term = jnp.dot(norm_second.T, grad_hidden, preferred_element_type=F32)

    grad_attended = jnp.dot(full_grads, attn_out_weight.T, preferred_element_type=F32)
    attended_b, grad_query, grad_key, grad_value = attention(
        query_b,
        grad_attended.reshape(seq_count, seq_rows, head_width),
        key_value[0],
        key_value[1],
        query_pos,
        key_pos,
    )
    attended_b = attended_b.reshape(tok_rows, head_width)

    if ctx_count == 2:

        def to_owner(grad):
            return (grad[:, :seq_rows] + swap(grad[:, seq_rows:], "ctx", 1)).reshape(
                tok_rows, head_width
            )
    else:

        def to_owner(grad):
            shares = grad.reshape(seq_count, ctx_count, seq_rows, head_width).swapaxes(0, 1)
            return lax.psum_scatter(
                shares.reshape(ctx_count * tok_rows, head_width), "ctx", scatter_dimension=0, tiled=True
            )

    attn_out_term = jnp.dot(attended_b.T, full_grads, preferred_element_type=F32)
    branch_terms = jnp.dot(attended_b, attn_out_weight, preferred_element_type=F32) + jnp.dot(
        activated_b, mlp_out_weight, preferred_element_type=F32
    )
    half = mlp_in_term.shape[0] // 2
    branch_sum, (mlp_out_grad, mlp_in_first), _ = sums(
        branch_terms, [mlp_out_term, mlp_in_term[:half]], 1
    )
    bias_rows = out_bias.astype(F32)
    mixed = (tokens.astype(F32) + branch_sum + bias_rows[0] + bias_rows[1]).astype(BF16)

    second_part = jnp.dot(grad_hidden, mlp_in_weight.T, preferred_element_type=F32)
    grad_proj = [
        rotate(0.125 * grad_query.reshape(tok_rows, head_width), tables, -1.0).astype(BF16),
        rotate(to_owner(grad_key), tables, -1.0).astype(BF16),
        to_owner(grad_value).astype(BF16),
    ]
    grad_proj = lax.optimization_barrier(jnp.concatenate(grad_proj, axis=1))
    qkv_term = jnp.dot(grad_proj.T, norm_first, preferred_element_type=F32)
    flat_weight = qkv_weight.transpose(1, 0, 2).reshape(qkv_weight.shape[1], 3 * head_width)
    first_part = jnp.dot(grad_proj, flat_weight.T, preferred_element_type=F32)

    combined = first_part * gains[0] + second_part * gains[1]
    features = full_tokens.shape[1]
    norm_term = jnp.stack(
        [
            jnp.sum(first_part * normed, axis=0),
            jnp.sum(second_part * normed, axis=0),
            jnp.sum(first_part, axis=0),
            jnp.sum(second_part, axis=0),
        ]
    )
    bias_term = jnp.concatenate(
        [
            jnp.sum(grad_proj.astype(F32), axis=0),
            jnp.sum(grad_local, axis=0),
            jnp.sum(grad_hidden.astype(F32), axis=0),
        ]
    )
    row_term = jnp.stack([jnp.sum(combined, axis=1), jnp.sum(combined * normed, axis=1)])
    bias_count = bias_term.shape[0]
    across = max(features, tok_rows, (bias_count + 1) // 2)
    small = jnp.concatenate(
        [
            jnp.pad(norm_term, ((0, 0), (0, across - features))),
            jnp.pad(bias_term, (0, 2 * across - bias_count)).reshape(2, across),
            jnp.pad(row_term, ((0, 0), (0, across - tok_rows))),
        ]
    )
    back_sum, (mlp_in_second, attn_out_grad, qkv_grad), small = sums(
        combined, [mlp_in_term[half:], attn_out_term, qkv_term], 2, small
    )
    mlp_in_grad = jnp.concatenate([mlp_in_first, mlp_in_second], axis=0)
    means = small[6:8, :tok_rows] * (1.0 / features)
    own_normed = lax.dynamic_slice_in_dim(normed, column_start, local_width, 1)
    input_grad = grad_local + inverse_scale * (
        back_sum - means[0][:, None] - own_normed * means[1][:, None]
    )
    norm_sum = lax.dynamic_slice_in_dim(small[:4, :features], column_start, local_width, 1)
    bias_sum = small[4:6].reshape(-1)[:bias_count]
    out_bias_grad = bias_sum[3 * head_width : 3 * head_width + local_width]
    return (
        mixed,
        input_grad,
        norm_sum[0:2],
        norm_sum[2:4],
        qkv_grad.reshape(3, head_width, -1).transpose(0, 2, 1),
        bias_sum[: 3 * head_width].reshape(3, head_width),
        attn_out_grad,
        jnp.stack([out_bias_grad, out_bias_grad]),
        mlp_in_grad,
        bias_sum[3 * head_width + local_width :],
        mlp_out_grad,
    )


def solution(mesh):
    placed = (
        P(("dp", "ctx"), "tensor"),
        P(),
        P(),
        P(),
        P(None, None, "tensor"),
        P(None, "tensor"),
        P("tensor", None),
        P(None, "tensor"),
        P(None, "tensor"),
        P("tensor"),
        P("tensor", None),
        P(("dp", "ctx"), "tensor"),
    )
    return jax.shard_map(
        local,
        mesh=mesh,
        in_specs=placed,
        out_specs=(
            P(("dp", "ctx"), "tensor"),
            P(("dp", "ctx"), "tensor"),
            P(None, "tensor"),
            P(None, "tensor"),
            P(None, None, "tensor"),
            P(None, "tensor"),
            P("tensor", None),
            P(None, "tensor"),
            P(None, "tensor"),
            P("tensor"),
            P("tensor", None),
        ),
        check_vma=False,
    )
```

```python
import functools

import jax
import jax.numpy as jnp
from jax import lax
from jax.experimental import pallas as pl
from jax.experimental.pallas import tpu as pltpu
from jax.sharding import PartitionSpec as P

HEAD = 64
ROT = 16
LEN = 2048
BF16 = jnp.bfloat16
F32 = jnp.float32


VMEM = pl.BlockSpec(memory_space=pltpu.VMEM)


def greet(partners):
    barrier = pltpu.get_barrier_semaphore()
    expected = 0
    for exists, device in partners:
        if exists is True:
            pl.semaphore_signal(barrier, inc=1, device_id=device)
            expected = expected + 1
        else:

            @pl.when(exists)
            def _():
                pl.semaphore_signal(barrier, inc=1, device_id=device)

            expected = expected + exists.astype(jnp.int32)
    pl.semaphore_wait(barrier, expected)


def line_partners(size, me):
    return [(me > 0, {"tensor": me - 1}), (me < size - 1, {"tensor": me + 1})]


def gather_body(size, pieces, *refs):
    arrays = (len(refs) - 5) // 2
    blocks, wholes = refs[:arrays], refs[arrays : 2 * arrays]
    up_send, up_recv, down_send, down_recv, own_sem = refs[2 * arrays :]
    me = lax.axis_index("tensor")
    rows, width = blocks[0].shape
    rows = rows // pieces
    greet(line_partners(size, me))

    def place(array, owner, piece):
        columns = pl.ds(pl.multiple_of(owner * width, width), width)
        return wholes[array].at[pl.ds(piece * rows, rows), columns]

    def copy(array, piece, step, sign):
        slot = (array * pieces + piece, step)
        send, recv = (up_send, up_recv) if sign > 0 else (down_send, down_recv)
        target = place(array, me - sign * step, piece)
        source = blocks[array].at[pl.ds(piece * rows, rows)] if step == 0 else target
        return pltpu.make_async_remote_copy(
            src_ref=source,
            dst_ref=target,
            send_sem=send.at[slot],
            recv_sem=recv.at[slot],
            device_id={"tensor": me + sign},
        )

    def arrival(array, piece, step, sign):
        slot = (array * pieces + piece, step)
        send, recv = (up_send, up_recv) if sign > 0 else (down_send, down_recv)
        target = place(array, me - sign * (step + 1), piece)
        return pltpu.make_async_remote_copy(
            src_ref=target,
            dst_ref=target,
            send_sem=send.at[slot],
            recv_sem=recv.at[slot],
            device_id={"tensor": me - sign},
        )

    own = [
        pltpu.make_async_copy(
            blocks[a], wholes[a].at[:, pl.ds(pl.multiple_of(me * width, width), width)], own_sem.at[a]
        )
        for a in range(arrays)
    ]
    for step in range(size):
        for array in range(arrays):
            for piece in range(pieces):
                if step:

                    @pl.when(me >= step)
                    def _():
                        arrival(array, piece, step - 1, 1).wait_recv()

                if step < size - 1:

                    @pl.when((me >= step) & (me < size - 1))
                    def _():
                        copy(array, piece, step, 1).start()

                if step:

                    @pl.when(me + step <= size - 1)
                    def _():
                        arrival(array, piece, step - 1, -1).wait_recv()

                if step < size - 1:

                    @pl.when((me + step <= size - 1) & (me > 0))
                    def _():
                        copy(array, piece, step, -1).start()

        if step == 0:
            for mine in own:
                mine.start()
    for mine in own:
        mine.wait()
    for step in range(size - 1):
        for array in range(arrays):
            for piece in range(pieces):

                @pl.when((me >= step) & (me < size - 1))
                def _():
                    copy(array, piece, step, 1).wait_send()

                @pl.when((me + step <= size - 1) & (me > 0))
                def _():
                    copy(array, piece, step, -1).wait_send()


def line_gather(*blocks):
    size, count = lax.axis_size("tensor"), len(blocks)
    rows, width = blocks[0].shape
    pieces = 4
    sems = pltpu.SemaphoreType.DMA((count * pieces, size - 1))
    whole = jax.ShapeDtypeStruct((rows, size * width), BF16)
    return pl.pallas_call(
        functools.partial(gather_body, size, pieces),
        in_specs=[VMEM] * count,
        out_specs=[VMEM] * count,
        out_shape=[whole] * count,
        scratch_shapes=[sems, sems, sems, sems, pltpu.SemaphoreType.DMA((count,))],
        compiler_params=pltpu.CompilerParams(
            collective_id=0, has_side_effects=True, vmem_limit_bytes=12 * 2**20
        ),
    )(*blocks)


def sum_body(size, pieces, groups, small_steps, *refs):
    if small_steps:
        small_in, small_out, refs = refs[0], refs[1], refs[2:]
        small_sum, small_land, small_sem, refs = refs[-3], refs[-2], refs[-1], refs[:-3]
    if groups:
        terms, shares, total, summed = refs[:4]
        core_in, low, chip_in = refs[-3:]
        line, (core_sem, chip_sem, back_sem, last_sem) = refs[4:10], refs[10:14]
    else:
        terms, total = refs[:2]
        line = refs[2:8]
    up_out, up_in, down_out, down_in, line_send, line_recv = line
    me = lax.axis_index("tensor")
    rows, width = total.shape
    rows = rows // pieces
    core, chip = lax.axis_index("ctx"), lax.axis_index("dp")
    partners = [(True, {"tensor": lax.rem(me + k, size)}) for k in range(1, size)]
    if groups:
        partners += [(True, {"ctx": 1 - core})]
        partners += [(True, {"dp": chip ^ bit}) for bit in range(1, groups)]
    elif small_steps:
        partners += [
            (True, {axis: lax.axis_index(axis) ^ bit}) for axis, bit in small_steps if axis != "tensor"
        ]
    greet(partners)

    def small_copy(step):
        axis, bit = small_steps[step]
        return pltpu.make_async_remote_copy(
            src_ref=small_sum.at[step], dst_ref=small_land.at[step],
            send_sem=small_sem.at[0, step], recv_sem=small_sem.at[1, step],
            device_id={axis: lax.axis_index(axis) ^ bit},
        )

    waiting = list(range(len(small_steps)))

    def small_next():
        if not waiting:
            return
        step = waiting.pop(0)
        small_copy(step).wait_recv()
        row = lax.broadcasted_iota(jnp.int32, small_in.shape, 0)
        counts = (row < 4) | (row >= 6) if small_steps[step][0] == "tensor" else row < 6
        small_sum[step + 1] = small_sum[step] + jnp.where(counts, small_land[step], 0.0)
        if waiting:
            small_copy(step + 1).start()
        else:
            small_out[...] = small_sum[step + 1]

    if small_steps:
        small_sum[0] = small_in[...]
        small_copy(0).start()

    def to_core(source, target, sem, slot):
        return pltpu.make_async_remote_copy(
            src_ref=source, dst_ref=target, send_sem=sem.at[0, slot], recv_sem=sem.at[1, slot],
            device_id={"ctx": 1 - core},
        )

    def to_chip(source, target, sem, bit):
        return pltpu.make_async_remote_copy(
            src_ref=source, dst_ref=target, send_sem=sem.at[0, bit - 1], recv_sem=sem.at[1, bit - 1],
            device_id={"dp": chip ^ bit},
        )

    def columns(owner, piece):
        at = pl.ds(pl.multiple_of(owner * width, width), width)
        return terms[pl.ds(piece * rows, rows), at]

    def line_copy(way, step, piece):
        out, into = (up_out, up_in) if way == 0 else (down_out, down_in)
        part = pl.ds(piece * rows, rows)
        slot = (way, (step - 1) * pieces + piece)
        return pltpu.make_async_remote_copy(
            src_ref=out.at[step - 1, part],
            dst_ref=into.at[step - 1, part],
            send_sem=line_send.at[slot],
            recv_sem=line_recv.at[slot],
            device_id={"tensor": me + 1 - 2 * way},
        )

    def sends(way, step):
        place = me if way == 0 else size - 1 - me
        return (place <= step - 1) & (place < size - 1)

    def line_step(step):
        reach = size - step
        for piece in range(pieces):
            part = pl.ds(piece * rows, rows)
            for way in range(2):
                out, into = (up_out, up_in) if way == 0 else (down_out, down_in)
                place = me if way == 0 else size - 1 - me
                owner = me + reach if way == 0 else me - reach

                @pl.when(sends(way, step) & (place == 0))
                def _():
                    out[step - 1, part] = columns(owner, piece)
                    line_copy(way, step, piece).start()

                if step > 1:

                    @pl.when(sends(way, step) & (place > 0))
                    def _():
                        line_copy(way, step - 1, piece).wait_recv()
                        value = columns(owner, piece).astype(F32) + into[step - 2, part].astype(F32)
                        out[step - 1, part] = value.astype(BF16)
                        line_copy(way, step, piece).start()

    orders = list(range(1, groups)) + [0] if groups else []
    for bit in orders:
        share = chip ^ bit
        to_core(shares.at[1 - core, share], core_in.at[share], core_sem, bit).start()
    line_step(1)
    for bit in orders[:-1]:
        share = chip ^ bit
        to_core(shares.at[1 - core, share], core_in.at[share], core_sem, bit).wait_recv()
        low[bit - 1] = (shares[core, share].astype(F32) + core_in[share].astype(F32)).astype(BF16)
        to_chip(low.at[bit - 1], chip_in.at[bit - 1], chip_sem, bit).start()
        small_next()
    for step in range(2, size):
        line_step(step)
        small_next()
    while waiting:
        small_next()
    if groups:
        to_core(shares.at[1 - core, chip], core_in.at[chip], core_sem, 0).wait_recv()
        for bit in range(1, groups):
            to_chip(low.at[bit - 1], chip_in.at[bit - 1], chip_sem, bit).wait_recv()
        own = shares[core, chip].astype(F32) + core_in[chip].astype(F32)
        for bit in range(1, groups):
            own = own + chip_in[bit - 1].astype(F32)
        summed[core, chip] = own.astype(BF16)
        for bit in range(1, groups):
            to_chip(summed.at[core, chip], summed.at[core, chip], back_sem, bit).start()
        to_core(summed.at[core, chip], summed.at[core, chip], last_sem, 0).start()

    for piece in range(pieces):
        part = pl.ds(piece * rows, rows)
        total[part] = columns(me, piece).astype(F32)
        for way in range(2):
            into = up_in if way == 0 else down_in
            place = me if way == 0 else size - 1 - me

            @pl.when(place > 0)
            def _():
                line_copy(way, size - 1, piece).wait_recv()
                total[part] += into[size - 2, part].astype(F32)

    if groups:
        for bit in range(1, groups):
            here = summed.at[core, chip ^ bit]
            to_chip(here, here, back_sem, bit).wait_recv()
            to_core(here, here, last_sem, bit).start()
        for bit in range(groups):
            there = summed.at[1 - core, chip ^ bit]
            to_core(there, there, last_sem, bit).wait_recv()
        for bit in range(groups):
            share, here = chip ^ bit, summed.at[core, chip ^ bit]
            to_core(shares.at[1 - core, share], core_in.at[share], core_sem, bit).wait_send()
            to_core(here, here, last_sem, bit).wait_send()
            if bit:
                to_chip(low.at[bit - 1], chip_in.at[bit - 1], chip_sem, bit).wait_send()
                own_place = summed.at[core, chip]
                to_chip(own_place, own_place, back_sem, bit).wait_send()
    for step in range(len(small_steps)):
        small_copy(step).wait_send()
    for step in range(1, size):
        for piece in range(pieces):
            for way in range(2):

                @pl.when(sends(way, step))
                def _():
                    line_copy(way, step, piece).wait_send()


def sums(terms, weights, number, small=None):
    size, spans, groups = lax.axis_size("tensor"), lax.axis_size("ctx"), lax.axis_size("dp")
    together = spans == 2 and groups & (groups - 1) == 0
    rows, width = terms.shape[0], terms.shape[1] // size
    pieces = 4
    passing = pltpu.VMEM((size - 1, rows, width), BF16)
    line_sems = pltpu.SemaphoreType.DMA((2, (size - 1) * pieces))
    scratch = [passing, passing, passing, passing, line_sems, line_sems]
    operands = [terms.astype(BF16)]
    shapes = [jax.ShapeDtypeStruct((rows, width), F32)]
    if together:
        joined = jnp.concatenate([w.astype(BF16) for w in weights], axis=0)
        depth, across = joined.shape
        shares = joined.reshape(spans, groups, depth // (spans * groups), across)
        operands.append(shares)
        shapes.append(jax.ShapeDtypeStruct(shares.shape, BF16))
        whole_sem = pltpu.SemaphoreType.DMA((2, groups))
        chip_sem = pltpu.SemaphoreType.DMA((2, groups - 1))
        part = shares.shape[2:]
        scratch += [
            whole_sem, chip_sem, chip_sem, whole_sem,
            pltpu.VMEM((groups, *part), BF16),
            pltpu.VMEM((groups - 1, *part), BF16),
            pltpu.VMEM((groups - 1, *part), BF16),
        ]
    small_steps = []
    if small is not None:
        for axis in ("tensor", "ctx", "dp"):
            bit = 1
            while bit < lax.axis_size(axis):
                small_steps.append((axis, bit))
                bit *= 2
        count = len(small_steps)
        operands = [small] + operands
        shapes = [jax.ShapeDtypeStruct(small.shape, F32)] + shapes
        scratch += [
            pltpu.VMEM((count + 1, *small.shape), F32),
            pltpu.VMEM((count, *small.shape), F32),
            pltpu.SemaphoreType.DMA((2, count)),
        ]
    body = functools.partial(sum_body, size, pieces, groups if together else 0, small_steps)
    if small is not None:
        plain, ins = body, len(operands)

        def body(*refs):
            plain(refs[0], refs[ins], *refs[1:ins], *refs[ins + 1 :])

    results = pl.pallas_call(
        body,
        in_specs=[VMEM] * len(operands),
        out_specs=[VMEM] * len(shapes),
        out_shape=shapes,
        scratch_shapes=scratch,
        compiler_params=pltpu.CompilerParams(
            collective_id=number, has_side_effects=True, vmem_limit_bytes=28 * 2**20
        ),
    )(*operands)
    shared = None
    if small is not None:
        shared, results = results[0], results[1:]
    if not together:
        return results[0], [lax.psum(w, ("dp", "ctx")) for w in weights], shared
    flat = results[1].reshape(depth, across)
    split, at = [], 0
    for w in weights:
        split.append(flat[at : at + w.shape[0]].astype(F32))
        at += w.shape[0]
    return results[0], split, shared


def swap(block, axis, bit):
    return lax.ppermute(block, axis, [(i, i ^ bit) for i in range(lax.axis_size(axis))])


def attention_body(
    heads, chunk, qmax, kmin, q, g, k, v, qpos, kpos, att, dq, dk, dv, e_keep, mass, out, k_head, v_head
):
    block = pl.program_id(1)
    width = q.shape[-1]
    chunks = k.shape[1] // chunk
    lane = lax.broadcasted_iota(jnp.int32, (1, width), 1)
    picks = [((lane >= h * HEAD) & (lane < (h + 1) * HEAD)).astype(F32) for h in range(heads)]

    @pl.when(block == 0)
    def _():
        dk[...] = jnp.zeros_like(dk)
        dv[...] = jnp.zeros_like(dv)
        for h in range(heads):
            k_head[h] = k[0] * picks[h].astype(BF16)
            v_head[h] = v[0] * picks[h].astype(BF16)

    nt = (((1,), (1,)), ((), ()))
    tn = (((0,), (0,)), ((), ()))
    dq[...] = jnp.zeros_like(dq)
    queries = q[0]
    grads = g[0]
    result = jnp.zeros(grads.shape, F32)
    for h in range(heads):
        mass[...] = jnp.zeros_like(mass)
        out[...] = jnp.zeros_like(out)
        for c in range(chunks):
            part = pl.ds(c * chunk, chunk)

            @pl.when(kmin[c] <= qmax[block])
            def _():
                raw = lax.dot_general(queries, k_head[h, part], nt, preferred_element_type=F32)
                e = jnp.where(kpos[:, part] <= qpos[...], jnp.exp(raw), 0.0)
                e_keep[:, part] = e
                mass[...] += jnp.sum(e, axis=1, keepdims=True)
                out[...] += jnp.dot(e.astype(BF16), v_head[h, part], preferred_element_type=F32)

        inverse = 1.0 / mass[...]
        attended = out[...] * inverse
        result = result + attended
        scaled = (grads * inverse).astype(BF16)
        corr = jnp.sum(grads * attended, axis=1, keepdims=True) * inverse
        pick = picks[h].astype(BF16)
        scaled_head = scaled * pick
        q_head = queries * pick
        for c in range(chunks):
            part = pl.ds(c * chunk, chunk)

            @pl.when(kmin[c] <= qmax[block])
            def _():
                e = e_keep[:, part]
                slope = lax.dot_general(scaled, v_head[h, part], nt, preferred_element_type=F32)
                d_raw = (e * (slope - corr)).astype(BF16)
                dq[0] += jnp.dot(d_raw, k_head[h, part], preferred_element_type=F32)
                dk[0, part] += lax.dot_general(d_raw, q_head, tn, preferred_element_type=F32)
                dv[0, part] += lax.dot_general(
                    e.astype(BF16), scaled_head, tn, preferred_element_type=F32
                )

    att[0] = result.astype(BF16)


def attention(q, g, k, v, qpos, kpos):
    seqs, q_rows, width = q.shape
    k_rows = k.shape[1]
    heads = width // HEAD
    block, chunk = min(512, q_rows), min(512, k_rows)
    qmax = jnp.max(qpos.reshape(-1, block), axis=1)
    kmin = jnp.min(kpos.reshape(-1, chunk), axis=1)
    by_block = pl.BlockSpec((1, block, width), lambda s, b: (s, b, 0))
    by_seq = pl.BlockSpec((1, k_rows, width), lambda s, b: (s, 0, 0))
    smem = pl.BlockSpec(memory_space=pltpu.SMEM)
    pairs = seqs * q_rows * k_rows * width
    return pl.pallas_call(
        functools.partial(attention_body, heads, chunk),
        grid=(seqs, q_rows // block),
        in_specs=[
            smem,
            smem,
            by_block,
            by_block,
            by_seq,
            by_seq,
            pl.BlockSpec((block, 1), lambda s, b: (b, 0)),
            pl.BlockSpec((1, k_rows), lambda s, b: (0, 0)),
        ],
        out_specs=[by_block, by_block, by_seq, by_seq],
        out_shape=[
            jax.ShapeDtypeStruct(q.shape, BF16),
            jax.ShapeDtypeStruct(q.shape, F32),
            jax.ShapeDtypeStruct(k.shape, F32),
            jax.ShapeDtypeStruct(k.shape, F32),
        ],
        scratch_shapes=[
            pltpu.VMEM((block, k_rows), F32),
            pltpu.VMEM((block, 1), F32),
            pltpu.VMEM((block, width), F32),
            pltpu.VMEM((heads, k_rows, width), BF16),
            pltpu.VMEM((heads, k_rows, width), BF16),
        ],
        cost_estimate=pl.CostEstimate(
            flops=48 * pairs, bytes_accessed=16 * seqs * k_rows * width, transcendentals=pairs // HEAD
        ),
        compiler_params=pltpu.CompilerParams(vmem_limit_bytes=38 * 2**20),
    )(qmax, kmin, q, g, k, v, qpos[:, None], kpos[None, :])


def norm_forward(full_rows):
    average = jnp.mean(full_rows, axis=-1, keepdims=True)
    centred = full_rows - average
    variance = jnp.mean(centred * centred, axis=-1, keepdims=True)
    inverse_scale = lax.rsqrt(variance + 1e-05)
    return (centred * inverse_scale, inverse_scale)


def rotation_tables(positions, width):
    half_rot = ROT // 2
    dim = jnp.arange(width, dtype=jnp.int32) % HEAD
    frequency = 10000.0 ** (-2.0 * (dim % half_rot).astype(F32) / ROT)
    angle = positions.astype(F32)[:, None] * frequency[None, :]
    cosine = jnp.where(dim < ROT, jnp.cos(angle), 1.0)
    sine = jnp.sin(angle)
    lower = jnp.where(dim < half_rot, sine, 0.0)
    upper = jnp.where((dim >= half_rot) & (dim < ROT), sine, 0.0)
    return lax.optimization_barrier((cosine, lower, upper))


def rotate(field, tables, sign):
    cosine, lower, upper = tables
    half_rot = ROT // 2
    return (
        field * cosine
        - sign * jnp.roll(field, -half_rot, axis=1) * lower
        + sign * jnp.roll(field, half_rot, axis=1) * upper
    )


def local(
    tokens,
    span_of_slot,
    norm_gain,
    norm_bias,
    qkv_weight,
    qkv_bias,
    attn_out_weight,
    out_bias,
    mlp_in_weight,
    mlp_in_bias,
    mlp_out_weight,
    cotangent,
):
    tok_rows, local_width = tokens.shape
    ctx_count = lax.axis_size("ctx")
    span_len = LEN // (2 * ctx_count)
    seq_count = tok_rows // (2 * span_len)
    seq_rows = 2 * span_len
    head_width = qkv_weight.shape[2]
    column_start = lax.axis_index("tensor") * local_width

    (full_tokens,) = line_gather(tokens)
    full_tokens, late_cotangent = lax.optimization_barrier((full_tokens, cotangent))
    full_grads = lax.all_gather(late_cotangent, "tensor", axis=1, tiled=True)

    slot_table = span_of_slot.reshape(ctx_count, 2)
    offsets = jnp.arange(span_len, dtype=jnp.int32)

    def positions_of(spans):
        return (spans[..., None] * span_len + offsets).reshape(-1)

    own_spans = lax.dynamic_index_in_dim(slot_table, lax.axis_index("ctx"), 0, False)
    query_pos = positions_of(own_spans)
    tables = rotation_tables(jnp.tile(query_pos, seq_count), head_width)

    normed, inverse_scale = norm_forward(full_tokens.astype(F32))
    gains = norm_gain.astype(F32)
    shifts = norm_bias.astype(F32)
    norm_first = (normed * gains[0] + shifts[0]).astype(BF16)
    norm_second = (normed * gains[1] + shifts[1]).astype(BF16)

    projected = [
        jnp.dot(norm_first, qkv_weight[c], preferred_element_type=F32) + qkv_bias[c].astype(F32)
        for c in range(3)
    ]
    query_b = (rotate(projected[0], tables, 1.0).astype(BF16) * BF16(0.125)).reshape(
        seq_count, seq_rows, head_width
    )
    key_value = jnp.stack([rotate(projected[1], tables, 1.0).astype(BF16), projected[2].astype(BF16)])
    if ctx_count == 2:
        other_spans = lax.dynamic_index_in_dim(slot_table, 1 - lax.axis_index("ctx"), 0, False)
        key_pos = positions_of(jnp.concatenate([own_spans, other_spans]))
        shards = [key_value, swap(key_value, "ctx", 1)]
    else:
        key_pos = positions_of(span_of_slot)
        shards = list(lax.all_gather(key_value, "ctx"))
    key_value = jnp.concatenate(
        [shard.reshape(2, seq_count, seq_rows, head_width) for shard in shards], axis=2
    )

    hidden = jnp.dot(norm_second, mlp_in_weight, preferred_element_type=F32) + mlp_in_bias.astype(F32)
    normal_cdf = 0.5 * (1.0 + lax.erf(hidden * 0.7071067811865476))
    density = jnp.exp(-0.5 * hidden * hidden) * 0.3989422804014327
    activated_b, gelu_slope = lax.optimization_barrier(
        ((hidden * normal_cdf).astype(BF16), normal_cdf + hidden * density)
    )

    grad_local = cotangent.astype(F32)
    mlp_out_term = jnp.dot(activated_b.T, full_grads, preferred_element_type=F32)
    grad_activated = jnp.dot(full_grads, mlp_out_weight.T, preferred_element_type=F32)
    grad_hidden = lax.optimization_barrier((grad_activated * gelu_slope).astype(BF16))
    mlp_in_term = jnp.dot(norm_second.T, grad_hidden, preferred_element_type=F32)

    grad_attended = jnp.dot(full_grads, attn_out_weight.T, preferred_element_type=F32)
    attended_b, grad_query, grad_key, grad_value = attention(
        query_b,
        grad_attended.reshape(seq_count, seq_rows, head_width),
        key_value[0],
        key_value[1],
        query_pos,
        key_pos,
    )
    attended_b = attended_b.reshape(tok_rows, head_width)

    if ctx_count == 2:

        def to_owner(grad):
            return (grad[:, :seq_rows] + swap(grad[:, seq_rows:], "ctx", 1)).reshape(
                tok_rows, head_width
            )
    else:

        def to_owner(grad):
            shares = grad.reshape(seq_count, ctx_count, seq_rows, head_width).swapaxes(0, 1)
            return lax.psum_scatter(
                shares.reshape(ctx_count * tok_rows, head_width), "ctx", scatter_dimension=0, tiled=True
            )

    attn_out_term = jnp.dot(attended_b.T, full_grads, preferred_element_type=F32)
    branch_terms = jnp.dot(attended_b, attn_out_weight, preferred_element_type=F32) + jnp.dot(
        activated_b, mlp_out_weight, preferred_element_type=F32
    )
    half = mlp_in_term.shape[0] // 2
    branch_sum, (mlp_out_grad, mlp_in_first), _ = sums(
        branch_terms, [mlp_out_term, mlp_in_term[:half]], 1
    )
    bias_rows = out_bias.astype(F32)
    mixed = (tokens.astype(F32) + branch_sum + bias_rows[0] + bias_rows[1]).astype(BF16)

    second_part = jnp.dot(grad_hidden, mlp_in_weight.T, preferred_element_type=F32)
    grad_proj = [
        rotate(0.125 * grad_query.reshape(tok_rows, head_width), tables, -1.0).astype(BF16),
        rotate(to_owner(grad_key), tables, -1.0).astype(BF16),
        to_owner(grad_value).astype(BF16),
    ]
    grad_proj = lax.optimization_barrier(jnp.concatenate(grad_proj, axis=1))
    qkv_term = jnp.dot(grad_proj.T, norm_first, preferred_element_type=F32)
    flat_weight = qkv_weight.transpose(1, 0, 2).reshape(qkv_weight.shape[1], 3 * head_width)
    first_part = jnp.dot(grad_proj, flat_weight.T, preferred_element_type=F32)

    combined = first_part * gains[0] + second_part * gains[1]
    features = full_tokens.shape[1]
    norm_term = jnp.stack(
        [
            jnp.sum(first_part * normed, axis=0),
            jnp.sum(second_part * normed, axis=0),
            jnp.sum(first_part, axis=0),
            jnp.sum(second_part, axis=0),
        ]
    )
    bias_term = jnp.concatenate(
        [
            jnp.sum(grad_proj.astype(F32), axis=0),
            jnp.sum(grad_local, axis=0),
            jnp.sum(grad_hidden.astype(F32), axis=0),
        ]
    )
    row_term = jnp.stack([jnp.sum(combined, axis=1), jnp.sum(combined * normed, axis=1)])
    bias_count = bias_term.shape[0]
    across = max(features, tok_rows, (bias_count + 1) // 2)
    small = jnp.concatenate(
        [
            jnp.pad(norm_term, ((0, 0), (0, across - features))),
            jnp.pad(bias_term, (0, 2 * across - bias_count)).reshape(2, across),
            jnp.pad(row_term, ((0, 0), (0, across - tok_rows))),
        ]
    )
    back_sum, (mlp_in_second, attn_out_grad, qkv_grad), small = sums(
        combined, [mlp_in_term[half:], attn_out_term, qkv_term], 2, small
    )
    mlp_in_grad = jnp.concatenate([mlp_in_first, mlp_in_second], axis=0)
    means = small[6:8, :tok_rows] * (1.0 / features)
    own_normed = lax.dynamic_slice_in_dim(normed, column_start, local_width, 1)
    input_grad = grad_local + inverse_scale * (
        back_sum - means[0][:, None] - own_normed * means[1][:, None]
    )
    norm_sum = lax.dynamic_slice_in_dim(small[:4, :features], column_start, local_width, 1)
    bias_sum = small[4:6].reshape(-1)[:bias_count]
    out_bias_grad = bias_sum[3 * head_width : 3 * head_width + local_width]
    return (
        mixed,
        input_grad,
        norm_sum[0:2],
        norm_sum[2:4],
        qkv_grad.reshape(3, head_width, -1).transpose(0, 2, 1),
        bias_sum[: 3 * head_width].reshape(3, head_width),
        attn_out_grad,
        jnp.stack([out_bias_grad, out_bias_grad]),
        mlp_in_grad,
        bias_sum[3 * head_width + local_width :],
        mlp_out_grad,
    )


def solution(mesh):
    placed = (
        P(("dp", "ctx"), "tensor"),
        P(),
        P(),
        P(),
        P(None, None, "tensor"),
        P(None, "tensor"),
        P("tensor", None),
        P(None, "tensor"),
        P(None, "tensor"),
        P("tensor"),
        P("tensor", None),
        P(("dp", "ctx"), "tensor"),
    )
    return jax.shard_map(
        local,
        mesh=mesh,
        in_specs=placed,
        out_specs=(
            P(("dp", "ctx"), "tensor"),
            P(("dp", "ctx"), "tensor"),
            P(None, "tensor"),
            P(None, "tensor"),
            P(None, None, "tensor"),
            P(None, "tensor"),
            P("tensor", None),
            P(None, "tensor"),
            P(None, "tensor"),
            P("tensor"),
            P("tensor", None),
        ),
        check_vma=False,
    )
```
